256 devices in a mesh: leaf: 64 (over z, y, core), head: 4 (over x).
Axes of the slice: x: 4, y: 4, z: 8, core: 2. Of those that a mesh axis runs over, the one named last changes fastest.
Arguments:
- queries: bfloat16 [32768, 4096], P('leaf', 'head'), may hold values from -180 to 180
- new_kv: bfloat16 [32768, 1024], P('leaf', 'head'), may hold values from -6 to 6
- prompt_kv: bfloat16 [1024, 1024], P('leaf', 'head'), may hold values from -6 to 6
- pool: bfloat16 [2048, 128, 1024], P('leaf', None, 'head'), may hold values from -6 to 6
- parents: int32 [256, 24], P('leaf'), may hold values from 0 to 2047, as said below
- lengths: int32 [256], P('leaf'), may hold values from 6 to 24, as said below
- location: int32 [2048], replicated, may hold values from 0 to 2047, as said below
- out_weight: bfloat16 [4096, 4096], P('head'), may hold values from -0.09375 to 0.09375
Outputs:
- mixed: bfloat16 [32768, 4096], P(('leaf', 'head'))
The draws below stay inside these ranges and needn't reach their ends.
Inputs may be any that keep to these rules, and one draw needn't show every extreme that they name: `parents`: segment numbers of stored segments; the ancestors of one segment are distinct. `parents`: the live slots of the segments of one index of leaf name at most 2 slots stored on any one index of leaf; this bound is reached in every draw. `lengths`: every draw has a segment with 24 live ancestors. Each storage row once; segment b is stored on index location[b] // 32 of leaf.
All inputs are finite; a program needn't handle non-finite values.
Results may differ from the reference program's by a relative error of at most 0.018.
Values may be sent and summed in bfloat16 or wider, within the bound.
No kernel may reach another device: no remote copies, remote signals or barrier semaphores. Data moves between devices by JAX's collectives and lax.ppermute only.
A program may use at most 128 MiB of HBM per device.

```python
import jax
import jax.numpy as jnp
from jax import lax

D = 4096
HD = 128
KVH = 4
GROUP = 8
SEG_LEN = 128
PROMPT = 1024
MAX_ANC = 24
SEG_DEV = 4
BLOCKS_DEV = 32
QHEADS = 32
SEGS = 256
TOKENS = 32768
POOL = 2048
N_LEAF = 64


def lineage_tables(key):
    first, second, third = jax.random.split(key, 3)
    slots = SEG_DEV * MAX_ANC
    capacity = max(2, (slots + N_LEAF - 1) // N_LEAF)
    groups = (slots + capacity - 1) // capacity
    slot_ids = jnp.arange(slots, dtype=jnp.int32)
    device_ids = jnp.arange(N_LEAF, dtype=jnp.int32)
    offsets = jax.random.randint(first, (N_LEAF, 1), 0, N_LEAF, dtype=jnp.int32)
    owner = (device_ids[:, None] + offsets + slot_ids[None, :] // capacity) % N_LEAF
    starts = jax.random.randint(second, (N_LEAF, groups), 0, BLOCKS_DEV, dtype=jnp.int32)
    base = jnp.take(starts, slot_ids // capacity, axis=1)
    stored = owner * BLOCKS_DEV + (base + slot_ids[None, :] % capacity) % BLOCKS_DEV
    location = jax.random.permutation(third, POOL).astype(jnp.int32)
    inverse = jnp.argsort(location, stable=True).astype(jnp.int32)
    logical = inverse[stored]
    parents = logical.reshape(SEGS, MAX_ANC).astype(jnp.int32)
    return (parents, location)


def prompt_values(key):
    return jnp.clip(jax.random.normal(jax.random.fold_in(key, 11), (PROMPT, KVH * 2 * HD), jnp.float32), -6.0, 6.0)


def draw_parents(key, part):
    tables = lineage_tables(key)
    return tables[0]


def draw_location(key, part):
    tables = lineage_tables(key)
    return tables[1]


def draw_lengths(key, part):
    key = jax.random.fold_in(key, 7)
    lowest = max(1, MAX_ANC // 4)
    drawn = jax.random.randint(key, (SEGS,), lowest, MAX_ANC + 1, dtype=jnp.int32)
    return drawn.at[:SEG_DEV].set(MAX_ANC)


def draw_prompt_kv(key, part):
    return prompt_values(key).astype(jnp.bfloat16)


def draw_queries(key, part):
    key = jax.random.fold_in(key, 3)
    base = jnp.clip(jax.random.normal(key, (TOKENS, KVH * GROUP * HD), jnp.float32), -6.0, 6.0)
    return base.astype(jnp.bfloat16)


def levels(own_key, extent, cuts, low, top_value):
    def one(axis_at, parts):
        heights = jax.random.uniform(jax.random.fold_in(jax.random.fold_in(own_key, 6), axis_at), (parts,), jnp.float32, low / len(cuts), top_value / len(cuts))
        return jnp.repeat(jnp.exp(heights), extent[axis_at] // parts).reshape((-1,) + (1,) * (len(extent) - axis_at - 1))

    loudness = one(*cuts[0])
    for cut in cuts[1:]:
        loudness = loudness * one(*cut)
    return loudness


def bell_draw(rng, shape, scale, most, pieces=(), kind=jnp.bfloat16):
    level = levels(rng, shape, pieces, -0.22, 0.18) if pieces else 1.0
    values = jax.random.normal(rng, shape, jnp.float32) * scale * level
    return jnp.minimum(jnp.maximum(values, -most), most).astype(kind)


def setup_inputs(seed: int = 0) -> dict:
    key_list = jax.random.split(jax.random.key(seed), 9)
    queries = draw_queries(jax.random.fold_in(key_list[8], 71), 0)
    new_kv = bell_draw(key_list[1], (TOKENS, KVH * 2 * HD), 1.0, 6.0, ((0, 64), (1, 4)))
    prompt_kv = draw_prompt_kv(jax.random.fold_in(key_list[8], 71), 0)
    pool = bell_draw(key_list[3], (POOL, SEG_LEN, KVH * 2 * HD), 1.0, 6.0, ((0, 64), (2, 4)))
    parents = draw_parents(jax.random.fold_in(key_list[8], 71), 0)
    lengths = draw_lengths(jax.random.fold_in(key_list[8], 71), 0)
    location = draw_location(jax.random.fold_in(key_list[8], 71), 0)
    out_weight = bell_draw(key_list[7], (QHEADS * HD, D), (QHEADS * HD) ** -0.5, 0.09375, ((0, 4),))
    return dict(queries=queries, new_kv=new_kv, prompt_kv=prompt_kv, pool=pool, parents=parents, lengths=lengths, location=location, out_weight=out_weight)


def one_segment(queries, new_kv, prompt_kv, pool, parents, lengths, location, index):
    start = (index * SEG_LEN).astype(jnp.int32)
    query = lax.dynamic_slice_in_dim(queries, start, SEG_LEN, 0).reshape(SEG_LEN, KVH, GROUP, HD)
    own = lax.dynamic_slice_in_dim(new_kv, start, SEG_LEN, 0)
    rows = location[parents[index]]
    ancestors = pool[rows].reshape(MAX_ANC * SEG_LEN, KVH * 2 * HD)
    whole = jnp.concatenate([prompt_kv, ancestors, own], axis=0).reshape(-1, KVH, 2, HD)
    keys = whole[:, :, 0, :].astype(jnp.float32)
    values = whole[:, :, 1, :].astype(jnp.float32)
    scores = jnp.einsum("qhgd,khd->hgqk", query.astype(jnp.float32), keys) * (HD ** -0.5)
    slot = jnp.arange(MAX_ANC * SEG_LEN) // SEG_LEN
    anc_live = slot < lengths[index]
    causal = jnp.arange(SEG_LEN)[:, None] >= jnp.arange(SEG_LEN)[None, :]
    visible = jnp.concatenate([jnp.ones((SEG_LEN, PROMPT), bool), jnp.broadcast_to(anc_live[None, :], (SEG_LEN, MAX_ANC * SEG_LEN)), causal], axis=1)
    masked = jnp.where(visible[None, None], scores, jnp.float32(-1e30))
    top = jnp.max(masked, axis=-1, keepdims=True)
    probs = jnp.where(visible[None, None], jnp.exp(masked - top), jnp.float32(0.0))
    total = jnp.sum(probs, axis=-1)
    weights = probs.astype(jnp.bfloat16).astype(jnp.float32)
    summed = jnp.einsum("hgqk,khd->hgqd", weights, values) / total[..., None]
    return jnp.transpose(summed, (2, 0, 1, 3)).reshape(SEG_LEN, KVH * GROUP * HD).astype(jnp.bfloat16)


def reference(queries, new_kv, prompt_kv, pool, parents, lengths, location, out_weight):
    def step(index):
        return one_segment(queries, new_kv, prompt_kv, pool, parents, lengths, location, index)

    attended = lax.map(step, jnp.arange(SEGS, dtype=jnp.int32)).reshape(TOKENS, KVH * GROUP * HD)
    return jnp.dot(attended, out_weight, preferred_element_type=jnp.float32).astype(jnp.bfloat16)
```

```python
import functools

import jax
import jax.numpy as jnp
from jax import lax
from jax.experimental import pallas as pl
from jax.experimental.pallas import tpu as pltpu
from jax.sharding import PartitionSpec as P

Y_SIZE = 4
CORES = 2
LANES = Y_SIZE * CORES
LOG2E = 1.4426950408889634
TILE = 256


def absorb(seg, keys, values, q_ref, m_ref, l_ref, acc_ref, scale, mask=None, first=False):
    factor = scale * LOG2E
    for at in range(0, q_ref.shape[2], TILE):
        cols = slice(at, at + TILE)
        scores = jnp.dot(keys, q_ref[seg, :, cols], preferred_element_type=jnp.float32)
        if mask is not None:
            scores = jnp.where(mask, scores, jnp.float32(-1e30))
        top = jnp.max(scores, axis=0, keepdims=True)
        if not first:
            before = m_ref[seg, :, cols]
            top = jnp.maximum(before, top)
        probs = jnp.exp2((scores - top) * factor)
        total = jnp.sum(probs, axis=0, keepdims=True)
        summed = lax.dot_general(
            values,
            probs.astype(jnp.bfloat16),
            (((0,), (0,)), ((), ())),
            preferred_element_type=jnp.float32,
        )
        if not first:
            shrink = jnp.exp2((before - top) * factor)
            total = total + l_ref[seg, :, cols] * shrink
            summed = summed + acc_ref[seg, :, cols] * shrink
        m_ref[seg, :, cols] = top
        l_ref[seg, :, cols] = total
        acc_ref[seg, :, cols] = summed


def absorb_blocks(seg_ref, blocks_ref, q_ref, m_ref, l_ref, acc_ref, list_ref, count_ref, scale):
    places = seg_ref.shape[0]
    segs = q_ref.shape[0]
    head_dim = q_ref.shape[1]
    for seg in range(segs):
        count_ref[seg] = 0

    def place(at, carry):
        seg = seg_ref[at]

        @pl.when(seg >= 0)
        def _():
            used = count_ref[seg]
            list_ref[seg * places + used] = at
            count_ref[seg] = used + 1

        return carry

    lax.fori_loop(0, places, place, 0)

    def per_segment(seg, carry):
        count = count_ref[seg]

        def pair(step, inner):
            one = list_ref[seg * places + 2 * step]
            two = list_ref[seg * places + 2 * step + 1]
            keys = jnp.concatenate(
                [blocks_ref[one, :, :head_dim], blocks_ref[two, :, :head_dim]], axis=0
            )
            values = jnp.concatenate(
                [blocks_ref[one, :, head_dim:], blocks_ref[two, :, head_dim:]], axis=0
            )
            absorb(seg, keys, values, q_ref, m_ref, l_ref, acc_ref, scale)
            return inner

        lax.fori_loop(0, count // 2, pair, 0)

        @pl.when(count % 2 == 1)
        def _():
            last = list_ref[seg * places + count - 1]
            absorb(
                seg,
                blocks_ref[last, :, :head_dim],
                blocks_ref[last, :, head_dim:],
                q_ref,
                m_ref,
                l_ref,
                acc_ref,
                scale,
            )

        return carry

    lax.fori_loop(0, segs, per_segment, 0)


def first_kernel(scale, seg_ref, q_ref, own_ref, blocks_ref, m_ref, l_ref, acc_ref, list_ref, count_ref):
    head_dim = q_ref.shape[1]
    seg_len = own_ref.shape[1]
    key_at = lax.broadcasted_iota(jnp.int32, (seg_len, TILE), 0)
    query_at = lax.broadcasted_iota(jnp.int32, (seg_len, TILE), 1) % seg_len
    causal = query_at >= key_at

    def own(seg, carry):
        absorb(
            seg,
            own_ref[seg, :, :head_dim],
            own_ref[seg, :, head_dim:],
            q_ref,
            m_ref,
            l_ref,
            acc_ref,
            scale,
            mask=causal,
            first=True,
        )
        return carry

    lax.fori_loop(0, q_ref.shape[0], own, 0)
    absorb_blocks(seg_ref, blocks_ref, q_ref, m_ref, l_ref, acc_ref, list_ref, count_ref, scale)


def carry_in(old, new):
    for source, target in zip(old, new):
        target[...] = source[...]


def prompt_kernel(scale, q_ref, prompt_ref, m_in, l_in, acc_in, m_ref, l_ref, acc_ref):
    head_dim = q_ref.shape[1]
    carry_in((m_in, l_in, acc_in), (m_ref, l_ref, acc_ref))

    def step(at, carry):
        seg = at % q_ref.shape[0]
        rows = pl.ds(pl.multiple_of((at // q_ref.shape[0]) * TILE, TILE), TILE)
        absorb(
            seg,
            prompt_ref[rows, :head_dim],
            prompt_ref[rows, head_dim:],
            q_ref,
            m_ref,
            l_ref,
            acc_ref,
            scale,
        )
        return carry

    lax.fori_loop(0, q_ref.shape[0] * (prompt_ref.shape[0] // TILE), step, 0)


def chunk_kernel(scale, seg_ref, q_ref, blocks_ref, m_in, l_in, acc_in, m_ref, l_ref, acc_ref, list_ref, count_ref):
    carry_in((m_in, l_in, acc_in), (m_ref, l_ref, acc_ref))
    absorb_blocks(seg_ref, blocks_ref, q_ref, m_ref, l_ref, acc_ref, list_ref, count_ref, scale)


def last_kernel(scale, seg_ref, q_ref, blocks_ref, m_in, l_in, acc_in, out_ref, m_ref, l_ref, acc_ref, list_ref, count_ref):
    carry_in((m_in, l_in, acc_in), (m_ref, l_ref, acc_ref))
    absorb_blocks(seg_ref, blocks_ref, q_ref, m_ref, l_ref, acc_ref, list_ref, count_ref, scale)
    seg_len = out_ref.shape[1]
    head_dim = q_ref.shape[1]
    group = q_ref.shape[2] // seg_len

    def finish(seg, carry):
        for g in range(group):
            cols = slice(g * seg_len, (g + 1) * seg_len)
            value = acc_ref[seg, :, cols] / l_ref[seg, :, cols]
            out_ref[seg, :, g * head_dim : (g + 1) * head_dim] = value.T.astype(jnp.bfloat16)
        return carry

    lax.fori_loop(0, q_ref.shape[0], finish, 0)


VMEM = pl.BlockSpec(memory_space=pltpu.VMEM)
SMEM = pl.BlockSpec(memory_space=pltpu.SMEM)


def state_shapes(q):
    segs, head_dim, columns = q.shape
    return [
        jax.ShapeDtypeStruct((segs, 1, columns), jnp.float32),
        jax.ShapeDtypeStruct((segs, 1, columns), jnp.float32),
        jax.ShapeDtypeStruct((segs, head_dim, columns), jnp.float32),
    ]


def cost(q, blocks):
    work = blocks * 128 * q.shape[2] * q.shape[1]
    return pl.CostEstimate(flops=8 * work, bytes_accessed=6 * q.size, transcendentals=work // 128)


def params():
    return pltpu.CompilerParams(vmem_limit_bytes=40 * 1024 * 1024)


def tables(places, segs):
    return [pltpu.SMEM((segs * places,), jnp.int32), pltpu.SMEM((segs,), jnp.int32)]


def attend_first(q, own, seg_of, blocks, scale):
    return pl.pallas_call(
        functools.partial(first_kernel, scale),
        out_shape=state_shapes(q),
        in_specs=[SMEM, VMEM, VMEM, VMEM],
        out_specs=[VMEM] * 3,
        scratch_shapes=tables(seg_of.shape[0], q.shape[0]),
        compiler_params=params(),
        cost_estimate=cost(q, 12),
    )(seg_of, q, own, blocks)


def attend_prompt(q, prompt, state, scale):
    return pl.pallas_call(
        functools.partial(prompt_kernel, scale),
        out_shape=state_shapes(q),
        in_specs=[VMEM] * 5,
        out_specs=[VMEM] * 3,
        compiler_params=params(),
        cost_estimate=cost(q, 32),
    )(q, prompt, *state)


def attend_chunk(q, seg_of, blocks, state, scale):
    return pl.pallas_call(
        functools.partial(chunk_kernel, scale),
        out_shape=state_shapes(q),
        in_specs=[SMEM] + [VMEM] * 5,
        out_specs=[VMEM] * 3,
        scratch_shapes=tables(seg_of.shape[0], q.shape[0]),
        compiler_params=params(),
        cost_estimate=cost(q, 16),
    )(seg_of, q, blocks, *state)


def attend_last(q, seg_of, blocks, state, scale):
    segs, head_dim, columns = q.shape
    seg_len = blocks.shape[1]
    group = columns // seg_len
    return pl.pallas_call(
        functools.partial(last_kernel, scale),
        out_shape=jax.ShapeDtypeStruct((segs, seg_len, group * head_dim), jnp.bfloat16),
        in_specs=[SMEM] + [VMEM] * 5,
        out_specs=VMEM,
        scratch_shapes=[pltpu.VMEM(s.shape, s.dtype) for s in state_shapes(q)]
        + tables(seg_of.shape[0], segs),
        compiler_params=params(),
        cost_estimate=cost(q, 8),
    )(seg_of, q, blocks, *state)


def per_device(queries, new_kv, prompt_kv, pool, parents, lengths, location, out_weight):
    tok_rows = queries.shape[0]
    seg_dev, max_anc = parents.shape
    head_dim = prompt_kv.shape[1] // 2
    group = queries.shape[1] // head_dim
    seg_len = tok_rows // seg_dev
    blocks = pool.shape[0]
    scale = head_dim ** (-0.5)
    n_leaf = lax.axis_size("leaf")
    planes = n_leaf // LANES
    capacity = 2
    me = lax.axis_index("leaf")
    plane = me // LANES

    def along_z(x, step):
        pairs = [(d, (d + step * LANES) % n_leaf) for d in range(n_leaf)]
        return lax.ppermute(x, "leaf", pairs)

    in_plane = [[p * LANES + lane for lane in range(LANES)] for p in range(planes)]

    def spread(x):
        return lax.all_to_all(x, "leaf", 0, 0, tiled=True, axis_index_groups=in_plane)

    up1 = along_z(pool, 1)
    down1 = along_z(pool, -1)

    prompt = lax.all_gather(prompt_kv, "leaf", axis=0, tiled=True)

    slots = seg_dev * max_anc
    stored = location[parents].reshape(-1)
    live = (jnp.arange(max_anc)[None, :] < lengths[:, None]).reshape(-1)
    owner = jnp.where(live, stored // blocks, -1)
    row = stored % blocks
    order = jnp.arange(slots)
    rank = jnp.sum(
        (owner[:, None] == owner[None, :]) & (order[:, None] > order[None, :]), axis=1
    )
    dist = (plane - owner // LANES) % planes
    cell = jnp.where(live, (dist * LANES + owner % LANES) * capacity + rank, -1)
    hit = cell[None, :] == jnp.arange(n_leaf * capacity)[:, None]
    wanted = jnp.sum(jnp.where(hit, row[None, :], 0), axis=1).astype(jnp.int32)
    seg_of = jnp.sum(jnp.where(hit, (order // max_anc + 1)[None, :], 0), axis=1) - 1
    seg_of = seg_of.astype(jnp.int32).reshape(planes, LANES, capacity)
    per_lane = jnp.transpose(wanted.reshape(planes, LANES, capacity), (1, 0, 2))
    ask = jnp.broadcast_to(
        per_lane.reshape(1, LANES, 1, planes * capacity), (planes, LANES, 1, planes * capacity)
    ).reshape(n_leaf, 1, planes * capacity)
    asked = lax.all_to_all(ask, "leaf", split_axis=0, concat_axis=0, tiled=True)
    asked = asked.reshape(planes, LANES, planes, capacity)
    asked = lax.dynamic_slice_in_dim(jnp.concatenate([asked, asked], axis=0), plane, planes, 0)
    here = asked[0]

    def pick(buffer, rows):
        return buffer[rows.reshape(-1)].reshape(rows.shape + buffer.shape[1:])

    def segs_at(dists):
        return jnp.stack([seg_of[d] for d in dists], axis=1).reshape(-1)

    def flat(x):
        return x.reshape((-1,) + x.shape[-2:])

    q = jnp.transpose(
        queries.reshape(seg_dev, seg_len, group, head_dim), (0, 3, 2, 1)
    ).reshape(seg_dev, head_dim, group * seg_len)
    own = new_kv.reshape(seg_dev, seg_len, 2 * head_dim)

    got0 = spread(pick(pool, here[:, 0]))
    state = attend_first(q, own, segs_at([0]), flat(got0), scale)

    up2 = along_z(up1, 1)
    down2 = along_z(down1, -1)
    got1 = spread(jnp.stack([pick(up1, here[:, 1]), pick(down1, here[:, planes - 1])], axis=1))
    state = attend_chunk(q, segs_at([1, planes - 1]), flat(got1), state, scale)

    state = attend_prompt(q, prompt, state, scale)

    half = LANES // 2
    far_up = pick(up2, asked[2, :half, 4])
    far_down = pick(down2, asked[planes - 2, half:, 4])
    near_up = pick(up2, asked[1, :, 3])
    near_down = pick(down2, asked[planes - 1, :, planes - 3])
    far_up3 = along_z(far_up, 1)
    far_down3 = along_z(far_down, -1)
    up3 = along_z(near_up, 1)
    down3 = along_z(near_down, -1)
    got2 = spread(jnp.stack([pick(up2, here[:, 2]), pick(down2, here[:, planes - 2])], axis=1))
    far_up4 = along_z(far_up3, 1)
    far_down4 = along_z(far_down3, -1)
    state = attend_chunk(q, segs_at([2, planes - 2]), flat(got2), state, scale)

    got3 = spread(jnp.stack([up3, down3], axis=1))
    state = attend_chunk(q, segs_at([3, planes - 3]), flat(got3), state, scale)

    got4 = spread(jnp.concatenate([far_up4, far_down4], axis=0))
    attended = attend_last(q, segs_at([4]), flat(got4), state, scale)

    return lax.psum_scatter(
        jnp.dot(
            attended.reshape(tok_rows, group * head_dim),
            out_weight,
            preferred_element_type=jnp.float32,
        ).astype(jnp.bfloat16),
        "head",
        scatter_dimension=0,
        tiled=True,
    )


def solution(mesh):
    return jax.shard_map(
        per_device,
        mesh=mesh,
        in_specs=(
            P("leaf", "head"),
            P("leaf", "head"),
            P("leaf", "head"),
            P("leaf", None, "head"),
            P("leaf", None),
            P("leaf"),
            P(),
            P("head", None),
        ),
        out_specs=P(("leaf", "head"), None),
        check_vma=False,
    )
```

```python
import functools

import jax
import jax.numpy as jnp
from jax import lax
from jax.experimental import pallas as pl
from jax.experimental.pallas import tpu as pltpu
from jax.sharding import PartitionSpec as P

Y_SIZE = 4
CORES = 2
LANES = Y_SIZE * CORES
LOG2E = 1.4426950408889634
TILE = 256
PROJECT_TILE = 2048
SMALL = pl.CostEstimate(flops=1 << 16, bytes_accessed=1 << 16, transcendentals=0)
LARGE = pl.CostEstimate(flops=0, bytes_accessed=1 << 31, transcendentals=0)


def absorb(seg, keys, values, q_ref, m_ref, l_ref, acc_ref, scale, mask=None, first=False):
    factor = scale * LOG2E
    tiles = [slice(at, at + TILE) for at in range(0, q_ref.shape[2], TILE)]
    scores = [jnp.dot(keys, q_ref[seg, :, t], preferred_element_type=jnp.float32) for t in tiles]
    if mask is not None:
        scores = [jnp.where(mask, x, jnp.float32(-1e30)) for x in scores]
    tops = [jnp.max(x, axis=0, keepdims=True) for x in scores]
    if not first:
        before = [m_ref[seg, :, t] for t in tiles]
        tops = [jnp.maximum(b, x) for b, x in zip(before, tops)]
        shrinks = [jnp.exp2((b - x) * factor) for b, x in zip(before, tops)]
    probs = [jnp.exp2((x - top) * factor) for x, top in zip(scores, tops)]
    totals = [jnp.sum(p, axis=0, keepdims=True) for p in probs]
    sums = [
        lax.dot_general(
            values,
            p.astype(jnp.bfloat16),
            (((0,), (0,)), ((), ())),
            preferred_element_type=jnp.float32,
        )
        for p in probs
    ]
    if not first:
        totals = [n + l_ref[seg, :, t] * f for n, t, f in zip(totals, tiles, shrinks)]
        sums = [n + acc_ref[seg, :, t] * f for n, t, f in zip(sums, tiles, shrinks)]
    for t, top, total, summed in zip(tiles, tops, totals, sums):
        m_ref[seg, :, t] = top
        l_ref[seg, :, t] = total
        acc_ref[seg, :, t] = summed


def absorb_blocks(seg_ref, blocks_ref, q_ref, m_ref, l_ref, acc_ref, list_ref, count_ref, scale):
    places = seg_ref.shape[0]
    segs = q_ref.shape[0]
    head_dim = q_ref.shape[1]
    for seg in range(segs):
        count_ref[seg] = 0

    def place(at, carry):
        seg = seg_ref[at]

        @pl.when(seg >= 0)
        def _():
            used = count_ref[seg]
            list_ref[seg * places + used] = at
            count_ref[seg] = used + 1

        return carry

    lax.fori_loop(0, places, place, 0)

    def per_segment(seg, carry):
        count = count_ref[seg]

        def take(at, how_many):
            places_of = [list_ref[seg * places + at + i] for i in range(how_many)]
            found = [blocks_ref[p] for p in places_of]
            both = found[0] if how_many == 1 else jnp.concatenate(found, axis=0)
            absorb(seg, both[:, :head_dim], both[:, head_dim:], q_ref, m_ref, l_ref, acc_ref, scale)

        def quad(step, inner):
            take(4 * step, 4)
            return inner

        lax.fori_loop(0, count // 4, quad, 0)
        rest = count // 4 * 4

        @pl.when(count % 4 >= 2)
        def _():
            take(rest, 2)

        @pl.when(count % 2 == 1)
        def _():
            take(count - 1, 1)

        return carry

    lax.fori_loop(0, segs, per_segment, 0)


def own_kernel(scale, q_ref, own_ref, m_ref, l_ref, acc_ref):
    head_dim = q_ref.shape[1]
    seg_len = own_ref.shape[1]
    key_at = lax.broadcasted_iota(jnp.int32, (seg_len, TILE), 0)
    query_at = lax.broadcasted_iota(jnp.int32, (seg_len, TILE), 1) % seg_len
    causal = query_at >= key_at

    def own(seg, carry):
        keys, values = own_ref[seg, :, :head_dim], own_ref[seg, :, head_dim:]
        absorb(seg, keys, values, q_ref, m_ref, l_ref, acc_ref, scale, mask=causal, first=True)
        return carry

    lax.fori_loop(0, q_ref.shape[0], own, 0)


def carry_in(old, new):
    for source, target in zip(old, new):
        target[...] = source[...]


def chunk_kernel(scale, shared, seg_ref, q_ref, blocks_ref, m_in, l_in, acc_in, m_ref, l_ref, acc_ref, list_ref, count_ref):
    carry_in((m_in, l_in, acc_in), (m_ref, l_ref, acc_ref))
    absorb_blocks(seg_ref, blocks_ref, q_ref, m_ref, l_ref, acc_ref, list_ref, count_ref, scale)
    head_dim = q_ref.shape[1]

    def step(seg, carry):
        for at in range(0, len(shared), 4):
            found = jnp.concatenate([blocks_ref[p] for p in shared[at : at + 4]], axis=0)
            keys, values = found[:, :head_dim], found[:, head_dim:]
            absorb(seg, keys, values, q_ref, m_ref, l_ref, acc_ref, scale)
        return carry

    if shared:
        lax.fori_loop(0, q_ref.shape[0], step, 0)


def last_kernel(scale, seg_ref, x_ref, q_ref, blocks_ref, m_in, l_in, acc_in, *refs):
    outs, (m_ref, l_ref, acc_ref, list_ref, count_ref) = refs[:-5], refs[-5:]
    carry_in((m_in, l_in, acc_in), (m_ref, l_ref, acc_ref))
    absorb_blocks(seg_ref, blocks_ref, q_ref, m_ref, l_ref, acc_ref, list_ref, count_ref, scale)
    seg_len = outs[0].shape[0]
    head_dim = q_ref.shape[1]
    group = q_ref.shape[2] // seg_len
    segs = q_ref.shape[0]

    for step, out_ref in enumerate(outs):
        seg = (x_ref[0] + step) % segs
        for g in range(group):
            cols = slice(g * seg_len, (g + 1) * seg_len)
            value = acc_ref[seg, :, cols] / l_ref[seg, :, cols]
            out_ref[:, g * head_dim : (g + 1) * head_dim] = value.T.astype(jnp.bfloat16)


def pick_kernel(sources, n_in, rows_ref, *refs):
    inputs, outputs, sems = refs[:n_in], refs[n_in:-1], refs[-1]
    base = 0
    for number, (names, out_ref) in enumerate(zip(sources, outputs)):

        def step(at, carry, names=names, out_ref=out_ref, base=base, number=number):
            for inner, name in enumerate(names):
                place = at * len(names) + inner
                pltpu.make_async_copy(
                    inputs[name].at[rows_ref[base + place]], out_ref.at[place], sems.at[number]
                ).start()
            return carry

        lax.fori_loop(0, out_ref.shape[0] // len(names), step, 0)
        base += out_ref.shape[0]
    for number, out_ref in enumerate(outputs):
        pltpu.make_async_copy(out_ref, out_ref, sems.at[number]).wait()


def project_kernel(kind, first, c_ref, *refs):
    out_ref = refs[-1]
    refs = list(refs[:-1])
    total = None if first else refs.pop(0)[...]
    if kind == "whole":
        pairs = [(refs[0][...], refs[1])]
    else:
        right, left = refs[0][...], refs[1][...]
        even = c_ref[0] == 0
        pairs = [(jnp.where(even, right, left), refs[2]), (jnp.where(even, left, right), refs[3])]
    for rows, weight_ref in pairs:
        product = jnp.dot(rows, weight_ref[...], preferred_element_type=jnp.float32)
        total = product if total is None else total + product
    out_ref[...] = total.astype(out_ref.dtype)


VMEM = pl.BlockSpec(memory_space=pltpu.VMEM)
SMEM = pl.BlockSpec(memory_space=pltpu.SMEM)
ANY = pl.BlockSpec(memory_space=pl.ANY)


def state_shapes(q):
    segs, head_dim, columns = q.shape
    return [
        jax.ShapeDtypeStruct((segs, 1, columns), jnp.float32),
        jax.ShapeDtypeStruct((segs, 1, columns), jnp.float32),
        jax.ShapeDtypeStruct((segs, head_dim, columns), jnp.float32),
    ]


def params():
    return pltpu.CompilerParams(vmem_limit_bytes=40 * 1024 * 1024)


def tables(places, segs):
    return [pltpu.SMEM((segs * places,), jnp.int32), pltpu.SMEM((segs,), jnp.int32)]


def attend_own(q, own, scale):
    return pl.pallas_call(
        functools.partial(own_kernel, scale),
        out_shape=state_shapes(q),
        in_specs=[VMEM, VMEM],
        out_specs=[VMEM] * 3,
        compiler_params=params(),
        cost_estimate=SMALL,
    )(q, own)


def attend_chunk(q, seg_of, blocks, state, scale, shared=()):
    return pl.pallas_call(
        functools.partial(chunk_kernel, scale, shared),
        out_shape=state_shapes(q),
        in_specs=[SMEM] + [VMEM] * 5,
        out_specs=[VMEM] * 3,
        scratch_shapes=tables(seg_of.shape[0], q.shape[0]),
        compiler_params=params(),
        cost_estimate=SMALL,
    )(seg_of, q, blocks, *state)


def attend_last(q, seg_of, blocks, state, x, scale):
    segs, head_dim, columns = q.shape
    seg_len = blocks.shape[1]
    group = columns // seg_len
    return pl.pallas_call(
        functools.partial(last_kernel, scale),
        out_shape=[jax.ShapeDtypeStruct((seg_len, group * head_dim), jnp.bfloat16)] * segs,
        in_specs=[SMEM, SMEM] + [VMEM] * 5,
        out_specs=[VMEM] * segs,
        scratch_shapes=[pltpu.VMEM(s.shape, s.dtype) for s in state_shapes(q)]
        + tables(seg_of.shape[0], segs),
        compiler_params=params(),
        cost_estimate=SMALL,
    )(seg_of, x, q, blocks, *state)


def pick(plan, buffers, told=None):
    block = buffers[0].shape[1:]
    out = pl.pallas_call(
        functools.partial(pick_kernel, tuple(names for names, _ in plan), len(buffers)),
        out_shape=[
            jax.ShapeDtypeStruct((rows.size,) + block, buffers[0].dtype) for _, rows in plan
        ],
        in_specs=[SMEM] + [ANY] * len(buffers),
        out_specs=[VMEM] * len(plan),
        scratch_shapes=[pltpu.SemaphoreType.DMA((len(plan),))],
        compiler_params=params(),
        cost_estimate=told or SMALL,
    )(jnp.concatenate([rows.reshape(-1) for _, rows in plan]), *buffers)
    return [x.reshape(rows.shape + block) for x, (_, rows) in zip(out, plan)]


def project(c, kind, blocks, weights, total, dtype):
    rows = blocks[0].shape[0]
    columns = weights[0].shape[1]
    tile = PROJECT_TILE
    wide = pl.BlockSpec((rows, tile), lambda at: (0, at))
    operands = [c] + ([] if total is None else [total]) + blocks + weights
    specs = [SMEM] + ([] if total is None else [wide])
    specs += [pl.BlockSpec(x.shape, lambda at: (0, 0)) for x in blocks]
    specs += [pl.BlockSpec((w.shape[0], tile), lambda at: (0, at)) for w in weights]
    depth = sum(w.shape[0] for w in weights)
    return pl.pallas_call(
        functools.partial(project_kernel, kind, total is None),
        out_shape=jax.ShapeDtypeStruct((rows, columns), dtype),
        grid=(columns // tile,),
        in_specs=specs,
        out_specs=wide,
        compiler_params=params(),
        cost_estimate=pl.CostEstimate(
            flops=2 * rows * depth * columns, bytes_accessed=2 * depth * columns, transcendentals=0
        ),
    )(*operands)


def together(*arrays):
    return lax.optimization_barrier(arrays)


def per_device(queries, new_kv, prompt_kv, pool, parents, lengths, location, out_weight):
    tok_rows = queries.shape[0]
    seg_dev, max_anc = parents.shape
    head_dim = prompt_kv.shape[1] // 2
    group = queries.shape[1] // head_dim
    seg_len = tok_rows // seg_dev
    blocks = pool.shape[0]
    scale = head_dim ** (-0.5)
    n_leaf = lax.axis_size("leaf")
    n_head = lax.axis_size("head")
    planes = n_leaf // LANES
    capacity = 2
    me = lax.axis_index("leaf")
    plane = me // LANES
    core = me % CORES

    def along_z(x, step):
        pairs = [(d, (d + step * LANES) % n_leaf) for d in range(n_leaf)]
        return lax.ppermute(x, "leaf", pairs)

    def along_x(x, step):
        return lax.ppermute(x, "head", [(d, (d + step) % n_head) for d in range(n_head)])

    def other_core(x):
        return lax.ppermute(x, "leaf", [(d, d ^ 1) for d in range(n_leaf)])

    in_plane = [[p * LANES + lane for lane in range(LANES)] for p in range(planes)]

    def spread(x):
        return lax.all_to_all(x, "leaf", 0, 0, tiled=True, axis_index_groups=in_plane)

    up1 = along_z(pool, 1)
    down1 = along_z(pool, -1)

    n_all = n_leaf * n_head

    def by_core(x):
        pairs = []
        for d in range(n_all):
            leaf, head = divmod(d, n_head)
            step = -1 if leaf % CORES == 0 else 1
            pairs.append((d, leaf * n_head + (head + step) % n_head))
        return lax.ppermute(x, ("leaf", "head"), pairs)

    weight1 = by_core(out_weight)

    slots = seg_dev * max_anc
    stored = location[parents].reshape(-1)
    live = (jnp.arange(max_anc)[None, :] < lengths[:, None]).reshape(-1)
    owner = jnp.where(live, stored // blocks, -1)
    row = stored % blocks
    order = jnp.arange(slots)
    rank = jnp.sum(
        (owner[:, None] == owner[None, :]) & (order[:, None] > order[None, :]), axis=1
    )
    dist = (plane - owner // LANES) % planes
    cell = jnp.where(live, (dist * LANES + owner % LANES) * capacity + rank, -1)
    hit = cell[None, :] == jnp.arange(n_leaf * capacity)[:, None]
    wanted = jnp.sum(jnp.where(hit, row[None, :], 0), axis=1).astype(jnp.int32)
    seg_of = jnp.sum(jnp.where(hit, (order // max_anc + 1)[None, :], 0), axis=1) - 1
    seg_of = seg_of.astype(jnp.int32).reshape(planes, LANES, capacity)
    per_lane = jnp.transpose(wanted.reshape(planes, LANES, capacity), (1, 0, 2))
    here = spread(per_lane.reshape(LANES, 1, planes * capacity))
    here = here.reshape(LANES, planes, capacity)

    q = jnp.transpose(
        queries.reshape(seg_dev, seg_len, group, head_dim), (0, 3, 2, 1)
    ).reshape(seg_dev, head_dim, group * seg_len)
    own = new_kv.reshape(seg_dev, seg_len, 2 * head_dim)
    state = attend_own(q, own, scale)
    here, *state = together(here, *state)

    def segs_at(dists, more=0):
        parts = [seg_of[d] for d in dists] + [jnp.full((LANES, more), -1, jnp.int32)] * bool(more)
        return jnp.concatenate(parts, axis=1).reshape(-1)

    def flat(x):
        return x.reshape((-1,) + x.shape[-2:])

    prompt_rows, width = prompt_kv.shape
    table = here.reshape(1, -1).astype(prompt_kv.dtype)
    table = jnp.pad(table, ((0, prompt_rows - 1), (0, width - table.shape[1])))
    notice = jnp.concatenate([prompt_kv, table], axis=0)
    same_lane = [[p * LANES + lane for p in range(planes)] for lane in range(LANES)]
    notices = lax.all_to_all(
        jnp.broadcast_to(notice[None], (planes,) + notice.shape),
        "leaf",
        0,
        0,
        tiled=True,
        axis_index_groups=same_lane,
    )
    up2 = along_z(up1, 1)
    down2 = along_z(down1, -1)
    lane_prompt = notices[:, :prompt_rows].reshape(1, planes * prompt_rows, width)
    asked = notices[:, prompt_rows, : LANES * planes * capacity].astype(jnp.int32)
    asked = asked.reshape(planes, LANES, planes, capacity)
    asked = lax.dynamic_slice_in_dim(jnp.concatenate([asked, asked], axis=0), plane, planes, 0)

    zero = jnp.zeros((LANES, 1), jnp.int32)
    rows01 = jnp.concatenate([here[:, 0], here[:, 1], here[:, planes - 1], zero], axis=1)
    plan01 = ((0, 0, 1, 1, 2, 2, 3), rows01)
    got01 = spread(pick([plan01], [pool, up1, down1, lane_prompt])[0])

    half = LANES // 2
    ask_up = jnp.concatenate([asked[1, :, 3], asked[2, :half, 4]], axis=0)
    ask_down = jnp.concatenate(
        [asked[planes - 1, :, planes - 3], asked[planes - 2, half:, 4]], axis=0
    )
    rows2 = jnp.concatenate([here[:, 2], here[:, planes - 2]], axis=1)
    send_up, send_down, rest = pick(
        [((0,), ask_up), ((1,), ask_down), ((0, 0, 1, 1), rows2)], [up2, down2], LARGE
    )
    up3 = along_z(send_up, 1)
    down3 = along_z(send_down, -1)
    rest, got01, weight1 = together(rest, got01, weight1)
    got2 = spread(rest)
    weight2 = by_core(weight1)
    weight1_too = other_core(weight1)
    every = 3 * capacity + 1
    prompts = tuple(range(every - 1, LANES * every, every))
    state = attend_chunk(
        q, segs_at([0, 1, planes - 1], 1), flat(got01), state, scale, shared=prompts
    )

    up3, down3, got2, *state = together(up3, down3, got2, *state)
    def counted(start, stop):
        return jnp.arange(start * capacity, stop * capacity, dtype=jnp.int32)

    in_turn = jnp.concatenate([counted(0, LANES).reshape(LANES, capacity)] * 2, axis=1)
    rest, far_up, far_down = pick(
        [
            ((0, 0, 1, 1), in_turn),
            ((0,), counted(LANES, LANES + half)),
            ((1,), counted(LANES, LANES + half)),
        ],
        [flat(up3), flat(down3)],
    )
    far_up4 = along_z(far_up, 1).reshape((half, capacity) + pool.shape[1:])
    far_down4 = along_z(far_down, -1).reshape((half, capacity) + pool.shape[1:])
    got3 = spread(rest)
    state = attend_chunk(q, segs_at([2, planes - 2]), flat(got2), state, scale)

    got4 = spread(jnp.concatenate([far_up4, far_down4], axis=0))
    state = attend_chunk(q, segs_at([3, planes - 3]), flat(got3), state, scale)

    got4, weight1_too, *state = together(got4, weight1_too, *state)
    x = lax.axis_index("head").astype(jnp.int32).reshape(1)
    keep, to_up, to_far, to_down = attend_last(q, segs_at([4]), flat(got4), state, x, scale)

    from_far = along_x(to_far, 2)
    from_down = along_x(to_up, 1)
    from_up = along_x(to_down, -1)
    c = core.astype(jnp.int32).reshape(1)
    total = project(c, "whole", [keep], [out_weight], None, jnp.float32)
    from_down, from_up, total = together(from_down, from_up, total)
    total = project(
        c, "either", [from_up, from_down], [weight1, weight1_too], total, jnp.float32
    )
    return project(c, "whole", [from_far], [weight2], total, jnp.bfloat16)


def solution(mesh):
    return jax.shard_map(
        per_device,
        mesh=mesh,
        in_specs=(
            P("leaf", "head"),
            P("leaf", "head"),
            P("leaf", "head"),
            P("leaf", None, "head"),
            P("leaf", None),
            P("leaf"),
            P(),
            P("head", None),
        ),
        out_specs=P(("leaf", "head"), None),
        check_vma=False,
    )
```

```python
import functools

import jax
import jax.numpy as jnp
from jax import lax
from jax.experimental import pallas as pl
from jax.experimental.pallas import tpu as pltpu
from jax.sharding import PartitionSpec as P

Y_SIZE = 4
CORES = 2
LANES = Y_SIZE * CORES
LOG2E = 1.4426950408889634
TILE = 256
PROJECT_TILE = 2048
SMALL = pl.CostEstimate(flops=1 << 16, bytes_accessed=1 << 16, transcendentals=0)
ATTEND = pl.CostEstimate(flops=1 << 35, bytes_accessed=1 << 16, transcendentals=0)
LARGE = pl.CostEstimate(flops=1 << 35, bytes_accessed=1 << 16, transcendentals=0)


def absorb(seg, keys, values, q_ref, m_ref, l_ref, acc_ref, scale, mask=None, first=False):
    factor = scale * LOG2E
    tiles = [slice(at, at + TILE) for at in range(0, q_ref.shape[2], TILE)]
    scores = [jnp.dot(keys, q_ref[seg, :, t], preferred_element_type=jnp.float32) for t in tiles]
    if mask is not None:
        scores = [jnp.where(mask, x, jnp.float32(-1e30)) for x in scores]
    tops = [jnp.max(x, axis=0, keepdims=True) for x in scores]
    if not first:
        before = [m_ref[seg, :, t] for t in tiles]
        tops = [jnp.maximum(b, x) for b, x in zip(before, tops)]
        shrinks = [jnp.exp2((b - x) * factor) for b, x in zip(before, tops)]
    probs = [jnp.exp2((x - top) * factor) for x, top in zip(scores, tops)]
    totals = [jnp.sum(p, axis=0, keepdims=True) for p in probs]
    sums = [
        lax.dot_general(
            values,
            p.astype(jnp.bfloat16),
            (((0,), (0,)), ((), ())),
            preferred_element_type=jnp.float32,
        )
        for p in probs
    ]
    if not first:
        totals = [n + l_ref[seg, :, t] * f for n, t, f in zip(totals, tiles, shrinks)]
        sums = [n + acc_ref[seg, :, t] * f for n, t, f in zip(sums, tiles, shrinks)]
    for t, top, total, summed in zip(tiles, tops, totals, sums):
        m_ref[seg, :, t] = top
        l_ref[seg, :, t] = total
        acc_ref[seg, :, t] = summed


def absorb_blocks(seg_ref, blocks_ref, q_ref, m_ref, l_ref, acc_ref, list_ref, count_ref, scale):
    places = seg_ref.shape[0]
    segs = q_ref.shape[0]
    head_dim = q_ref.shape[1]
    for seg in range(segs):
        count_ref[seg] = 0

    def place(at, carry):
        seg = seg_ref[at]

        @pl.when(seg >= 0)
        def _():
            used = count_ref[seg]
            list_ref[seg * places + used] = at
            count_ref[seg] = used + 1

        return carry

    lax.fori_loop(0, places, place, 0)

    def per_segment(seg, carry):
        count = count_ref[seg]

        def take(at, how_many):
            places_of = [list_ref[seg * places + at + i] for i in range(how_many)]
            found = [blocks_ref[p] for p in places_of]
            both = found[0] if how_many == 1 else jnp.concatenate(found, axis=0)
            absorb(seg, both[:, :head_dim], both[:, head_dim:], q_ref, m_ref, l_ref, acc_ref, scale)

        def quad(step, inner):
            take(4 * step, 4)
            return inner

        lax.fori_loop(0, count // 4, quad, 0)
        rest = count // 4 * 4

        @pl.when(count % 4 >= 2)
        def _():
            take(rest, 2)

        @pl.when(count % 2 == 1)
        def _():
            take(count - 1, 1)

        return carry

    lax.fori_loop(0, segs, per_segment, 0)


def own_kernel(scale, q_ref, own_ref, m_ref, l_ref, acc_ref):
    head_dim = q_ref.shape[1]
    seg_len = own_ref.shape[1]
    key_at = lax.broadcasted_iota(jnp.int32, (seg_len, TILE), 0)
    query_at = lax.broadcasted_iota(jnp.int32, (seg_len, TILE), 1) % seg_len
    causal = query_at >= key_at

    def own(seg, carry):
        keys, values = own_ref[seg, :, :head_dim], own_ref[seg, :, head_dim:]
        absorb(seg, keys, values, q_ref, m_ref, l_ref, acc_ref, scale, mask=causal, first=True)
        return carry

    lax.fori_loop(0, q_ref.shape[0], own, 0)


def carry_in(old, new):
    for source, target in zip(old, new):
        target[...] = source[...]


def chunk_kernel(scale, shared, seg_ref, q_ref, blocks_ref, m_in, l_in, acc_in, m_ref, l_ref, acc_ref, list_ref, count_ref):
    carry_in((m_in, l_in, acc_in), (m_ref, l_ref, acc_ref))
    absorb_blocks(seg_ref, blocks_ref, q_ref, m_ref, l_ref, acc_ref, list_ref, count_ref, scale)
    head_dim = q_ref.shape[1]

    def step(seg, carry):
        for at in range(0, len(shared), 4):
            found = jnp.concatenate([blocks_ref[p] for p in shared[at : at + 4]], axis=0)
            keys, values = found[:, :head_dim], found[:, head_dim:]
            absorb(seg, keys, values, q_ref, m_ref, l_ref, acc_ref, scale)
        return carry

    if shared:
        lax.fori_loop(0, q_ref.shape[0], step, 0)


def last_kernel(scale, seg_a_ref, seg_b_ref, x_ref, q_ref, blocks_a_ref, blocks_b_ref, m_in, l_in, acc_in, *refs):
    outs, (m_ref, l_ref, acc_ref, list_ref, count_ref) = refs[:-5], refs[-5:]
    carry_in((m_in, l_in, acc_in), (m_ref, l_ref, acc_ref))
    for seg_ref, blocks_ref in ((seg_a_ref, blocks_a_ref), (seg_b_ref, blocks_b_ref)):
        absorb_blocks(
            seg_ref, blocks_ref, q_ref, m_ref, l_ref, acc_ref, list_ref, count_ref, scale
        )
    seg_len = outs[0].shape[0]
    head_dim = q_ref.shape[1]
    group = q_ref.shape[2] // seg_len
    segs = q_ref.shape[0]

    for step, out_ref in enumerate(outs):
        seg = (x_ref[0] + step) % segs
        for g in range(group):
            cols = slice(g * seg_len, (g + 1) * seg_len)
            value = acc_ref[seg, :, cols] / l_ref[seg, :, cols]
            out_ref[:, g * head_dim : (g + 1) * head_dim] = value.T.astype(jnp.bfloat16)


def pick_kernel(sources, n_in, rows_ref, *refs):
    count = len(sources)
    inputs, outputs = refs[:n_in], refs[n_in : n_in + count]
    buffers, reads, write = refs[n_in + count : n_in + 2 * count], refs[-1 - count : -1], refs[-1]
    base = 0
    for names, buffer, read in zip(sources, buffers, reads):

        def start(at, carry, names=names, buffer=buffer, read=read, base=base):
            for inner, name in enumerate(names):
                place = at * len(names) + inner
                block = inputs[name].at[rows_ref[base + place]]
                pltpu.make_async_copy(block, buffer.at[place], read.at[at]).start()
            return carry

        lax.fori_loop(0, buffer.shape[0] // len(names), start, 0)
        base += buffer.shape[0]
    for number, (names, buffer, out_ref, read) in enumerate(zip(sources, buffers, outputs, reads)):

        def pass_on(at, carry, names=names, buffer=buffer, out_ref=out_ref, read=read, number=number):
            part = pl.ds(at * len(names), len(names))
            pltpu.make_async_copy(buffer.at[part], buffer.at[part], read.at[at]).wait()
            pltpu.make_async_copy(buffer.at[part], out_ref.at[part], write.at[number]).start()
            return carry

        lax.fori_loop(0, buffer.shape[0] // len(names), pass_on, 0)
    for number, (buffer, out_ref) in enumerate(zip(buffers, outputs)):
        pltpu.make_async_copy(buffer, out_ref, write.at[number]).wait()


def project_kernel(kind, first, c_ref, *refs):
    out_ref = refs[-1]
    refs = list(refs[:-1])
    total = None if first else refs.pop(0)[...]
    if kind == "whole":
        pairs = [(refs[0][...], refs[1])]
    else:
        right, left = refs[0][...], refs[1][...]
        even = c_ref[0] == 0
        pairs = [(jnp.where(even, right, left), refs[2]), (jnp.where(even, left, right), refs[3])]
    for rows, weight_ref in pairs:
        product = jnp.dot(rows, weight_ref[...], preferred_element_type=jnp.float32)
        total = product if total is None else total + product
    out_ref[...] = total.astype(out_ref.dtype)


VMEM = pl.BlockSpec(memory_space=pltpu.VMEM)
SMEM = pl.BlockSpec(memory_space=pltpu.SMEM)
ANY = pl.BlockSpec(memory_space=pl.ANY)


def state_shapes(q):
    segs, head_dim, columns = q.shape
    return [
        jax.ShapeDtypeStruct((segs, 1, columns), jnp.float32),
        jax.ShapeDtypeStruct((segs, 1, columns), jnp.float32),
        jax.ShapeDtypeStruct((segs, head_dim, columns), jnp.float32),
    ]


def params():
    return pltpu.CompilerParams(vmem_limit_bytes=40 * 1024 * 1024)


def tables(places, segs):
    return [pltpu.SMEM((segs * places,), jnp.int32), pltpu.SMEM((segs,), jnp.int32)]


def attend_own(q, own, scale):
    return pl.pallas_call(
        functools.partial(own_kernel, scale),
        out_shape=state_shapes(q),
        in_specs=[VMEM, VMEM],
        out_specs=[VMEM] * 3,
        compiler_params=params(),
        cost_estimate=SMALL,
    )(q, own)


def attend_chunk(q, seg_of, blocks, state, scale, shared=()):
    return pl.pallas_call(
        functools.partial(chunk_kernel, scale, shared),
        out_shape=state_shapes(q),
        in_specs=[SMEM] + [VMEM] * 5,
        out_specs=[VMEM] * 3,
        scratch_shapes=tables(seg_of.shape[0], q.shape[0]),
        compiler_params=params(),
        cost_estimate=ATTEND,
    )(seg_of, q, blocks, *state)


def attend_last(q, fetched, state, x, scale):
    (seg_a, blocks_a), (seg_b, blocks_b) = fetched
    segs, head_dim, columns = q.shape
    seg_len = blocks_a.shape[1]
    group = columns // seg_len
    places = max(seg_a.shape[0], seg_b.shape[0])
    return pl.pallas_call(
        functools.partial(last_kernel, scale),
        out_shape=[jax.ShapeDtypeStruct((seg_len, group * head_dim), jnp.bfloat16)] * segs,
        in_specs=[SMEM] * 3 + [VMEM] * 6,
        out_specs=[VMEM] * segs,
        scratch_shapes=[pltpu.VMEM(s.shape, s.dtype) for s in state_shapes(q)]
        + tables(places, segs),
        compiler_params=params(),
        cost_estimate=ATTEND,
    )(seg_a, seg_b, x, q, blocks_a, blocks_b, *state)


def pick(plan, buffers, told=None):
    block, dtype = buffers[0].shape[1:], buffers[0].dtype
    names = tuple(n for n, _ in plan)
    sizes = [rows.size for _, rows in plan]
    out = pl.pallas_call(
        functools.partial(pick_kernel, names, len(buffers)),
        out_shape=[jax.ShapeDtypeStruct((size,) + block, dtype) for size in sizes],
        in_specs=[SMEM] + [ANY] * len(buffers),
        out_specs=[ANY] * len(plan),
        scratch_shapes=[pltpu.VMEM((size,) + block, dtype) for size in sizes]
        + [pltpu.SemaphoreType.DMA((size // len(n),)) for n, size in zip(names, sizes)]
        + [pltpu.SemaphoreType.DMA((len(plan),))],
        compiler_params=pltpu.CompilerParams(vmem_limit_bytes=56 * 1024 * 1024),
        cost_estimate=told or SMALL,
    )(jnp.concatenate([rows.reshape(-1) for _, rows in plan]), *buffers)
    return [x.reshape(rows.shape + block) for x, (_, rows) in zip(out, plan)]


def project(c, kind, blocks, weights, total, dtype):
    rows = blocks[0].shape[0]
    columns = weights[0].shape[1]
    tile = PROJECT_TILE
    wide = pl.BlockSpec((rows, tile), lambda at: (0, at))
    operands = [c] + ([] if total is None else [total]) + blocks + weights
    specs = [SMEM] + ([] if total is None else [wide])
    specs += [pl.BlockSpec(x.shape, lambda at: (0, 0)) for x in blocks]
    specs += [pl.BlockSpec((w.shape[0], tile), lambda at: (0, at)) for w in weights]
    depth = sum(w.shape[0] for w in weights)
    return pl.pallas_call(
        functools.partial(project_kernel, kind, total is None),
        out_shape=jax.ShapeDtypeStruct((rows, columns), dtype),
        grid=(columns // tile,),
        in_specs=specs,
        out_specs=wide,
        compiler_params=params(),
        cost_estimate=pl.CostEstimate(
            flops=2 * rows * depth * columns, bytes_accessed=2 * depth * columns, transcendentals=0
        ),
    )(*operands)


def together(*arrays):
    return lax.optimization_barrier(arrays)


def per_device(queries, new_kv, prompt_kv, pool, parents, lengths, location, out_weight):
    tok_rows = queries.shape[0]
    seg_dev, max_anc = parents.shape
    head_dim = prompt_kv.shape[1] // 2
    group = queries.shape[1] // head_dim
    seg_len = tok_rows // seg_dev
    blocks = pool.shape[0]
    scale = head_dim ** (-0.5)
    n_leaf = lax.axis_size("leaf")
    n_head = lax.axis_size("head")
    planes = n_leaf // LANES
    capacity = 2
    me = lax.axis_index("leaf")
    plane = me // LANES
    core = me % CORES

    def along_z(x, step):
        pairs = [(d, (d + step * LANES) % n_leaf) for d in range(n_leaf)]
        return lax.ppermute(x, "leaf", pairs)

    def along_x(x, step):
        return lax.ppermute(x, "head", [(d, (d + step) % n_head) for d in range(n_head)])

    def other_core(x):
        return lax.ppermute(x, "leaf", [(d, d ^ 1) for d in range(n_leaf)])

    in_plane = [[p * LANES + lane for lane in range(LANES)] for p in range(planes)]

    def spread(x):
        return lax.all_to_all(x, "leaf", 0, 0, tiled=True, axis_index_groups=in_plane)

    up1 = along_z(pool, 1)
    down1 = along_z(pool, -1)

    n_all = n_leaf * n_head

    def by_core(x):
        pairs = []
        for d in range(n_all):
            leaf, head = divmod(d, n_head)
            step = -1 if leaf % CORES == 0 else 1
            pairs.append((d, leaf * n_head + (head + step) % n_head))
        return lax.ppermute(x, ("leaf", "head"), pairs)

    weight1 = by_core(out_weight)

    slots = seg_dev * max_anc
    stored = location[parents].reshape(-1)
    live = (jnp.arange(max_anc)[None, :] < lengths[:, None]).reshape(-1)
    owner = jnp.where(live, stored // blocks, -1)
    row = stored % blocks
    order = jnp.arange(slots)
    rank = jnp.sum(
        (owner[:, None] == owner[None, :]) & (order[:, None] > order[None, :]), axis=1
    )
    dist = (plane - owner // LANES) % planes
    cell = jnp.where(live, (dist * LANES + owner % LANES) * capacity + rank, -1)
    hit = cell[None, :] == jnp.arange(n_leaf * capacity)[:, None]
    wanted = jnp.sum(jnp.where(hit, row[None, :], 0), axis=1).astype(jnp.int32)
    seg_of = jnp.sum(jnp.where(hit, (order // max_anc + 1)[None, :], 0), axis=1) - 1
    seg_of = seg_of.astype(jnp.int32).reshape(planes, LANES, capacity)
    per_lane = jnp.transpose(wanted.reshape(planes, LANES, capacity), (1, 0, 2))
    here = spread(per_lane.reshape(LANES, 1, planes * capacity))
    here = here.reshape(LANES, planes, capacity)

    q = jnp.transpose(
        queries.reshape(seg_dev, seg_len, group, head_dim), (0, 3, 2, 1)
    ).reshape(seg_dev, head_dim, group * seg_len)
    own = new_kv.reshape(seg_dev, seg_len, 2 * head_dim)
    state = attend_own(q, own, scale)
    here, *state = together(here, *state)

    def segs_at(dists, more=0):
        parts = [seg_of[d] for d in dists] + [jnp.full((LANES, more), -1, jnp.int32)] * bool(more)
        return jnp.concatenate(parts, axis=1).reshape(-1)

    def flat(x):
        return x.reshape((-1,) + x.shape[-2:])

    prompt_rows, width = prompt_kv.shape
    table = here.reshape(1, -1).astype(prompt_kv.dtype)
    table = jnp.pad(table, ((0, prompt_rows - 1), (0, width - table.shape[1])))
    notice = jnp.concatenate([prompt_kv, table], axis=0)
    same_lane = [[p * LANES + lane for p in range(planes)] for lane in range(LANES)]
    notices = lax.all_to_all(
        jnp.broadcast_to(notice[None], (planes,) + notice.shape),
        "leaf",
        0,
        0,
        tiled=True,
        axis_index_groups=same_lane,
    )
    notices, up1, down1 = together(notices, up1, down1)
    up2 = along_z(up1, 1)
    down2 = along_z(down1, -1)
    lane_prompt = notices[:, :prompt_rows].reshape(1, planes * prompt_rows, width)
    asked = notices[:, prompt_rows, : LANES * planes * capacity].astype(jnp.int32)
    asked = asked.reshape(planes, LANES, planes, capacity)
    asked = lax.dynamic_slice_in_dim(jnp.concatenate([asked, asked], axis=0), plane, planes, 0)

    zero = jnp.zeros((LANES, 1), jnp.int32)
    rows01 = jnp.concatenate([here[:, 0], here[:, 1], here[:, planes - 1], zero], axis=1)
    plan01 = ((0, 0, 1, 1, 2, 2, 3), rows01)
    got01 = spread(pick([plan01], [pool, up1, down1, lane_prompt])[0])
    up2, down2, weight1 = together(up2, down2, weight1)
    weight2 = by_core(weight1)
    ask_up = asked[1, :, 3]
    ask_down = asked[planes - 1, :, planes - 3]
    on_core = (jnp.arange(LANES) % CORES)[:, None]
    ask_far = jnp.where(on_core == 0, asked[2, :, 4], asked[planes - 2, :, 4])
    rows2 = jnp.concatenate([here[:, 2], here[:, planes - 2], ask_far], axis=1)
    send_up, send_down, rest = pick(
        [
            ((0, 0), ask_up),
            ((1, 1), ask_down),
            ((0, 0, 1, 1, 0, 0, 0, 0, 1, 1, 1, 1), rows2),
        ],
        [up2, down2],
        LARGE,
    )
    up3 = along_z(send_up, 1)
    down3 = along_z(send_down, -1)
    rest, got01, weight1 = together(rest, got01, weight1)
    got2 = spread(rest)
    weight1_too = other_core(weight1)
    every = 3 * capacity + 1
    prompts = tuple(range(every - 1, LANES * every, every))
    state = attend_chunk(
        q, segs_at([0, 1, planes - 1], 1), flat(got01), state, scale, shared=prompts
    )

    up3, down3, *state = together(up3, down3, *state)
    reach = [(d, (d + (2 if d % CORES == 0 else -2) * LANES) % n_leaf) for d in range(n_leaf)]
    got4 = lax.ppermute(got2[:, 2 * capacity :], "leaf", reach)
    got3 = spread(jnp.concatenate([up3, down3], axis=1))
    state = attend_chunk(q, segs_at([2, planes - 2], capacity), flat(got2), state, scale)

    got3, got4, weight1_too, *state = together(got3, got4, weight1_too, *state)
    x = lax.axis_index("head").astype(jnp.int32).reshape(1)
    fetched = ((segs_at([3, planes - 3]), flat(got3)), (segs_at([4]), flat(got4)))
    keep, to_up, to_far, to_down = attend_last(q, fetched, state, x, scale)

    from_far = along_x(to_far, 2)
    from_down = along_x(to_up, 1)
    from_up = along_x(to_down, -1)
    c = core.astype(jnp.int32).reshape(1)
    total = project(c, "whole", [keep], [out_weight], None, jnp.float32)
    from_down, from_up, total = together(from_down, from_up, total)
    total = project(
        c, "either", [from_up, from_down], [weight1, weight1_too], total, jnp.float32
    )
    return project(c, "whole", [from_far], [weight2], total, jnp.bfloat16)


def solution(mesh):
    return jax.shard_map(
        per_device,
        mesh=mesh,
        in_specs=(
            P("leaf", "head"),
            P("leaf", "head"),
            P("leaf", "head"),
            P("leaf", None, "head"),
            P("leaf", None),
            P("leaf"),
            P(),
            P("head", None),
        ),
        out_specs=P(("leaf", "head"), None),
        check_vma=False,
    )
```

```python
import functools

import jax
import jax.numpy as jnp
from jax import lax
from jax.experimental import pallas as pl
from jax.experimental.pallas import tpu as pltpu
from jax.sharding import PartitionSpec as P

Y_SIZE = 4
CORES = 2
LANES = Y_SIZE * CORES
LOG2E = 1.4426950408889634
TILE = 256
PROJECT_TILE = 1024
SMALL = pl.CostEstimate(flops=1 << 16, bytes_accessed=1 << 16, transcendentals=0)
ATTEND = pl.CostEstimate(flops=1 << 35, bytes_accessed=1 << 16, transcendentals=0)
LARGE = pl.CostEstimate(flops=1 << 35, bytes_accessed=1 << 16, transcendentals=0)


def absorb(seg, keys, values, q_ref, m_ref, l_ref, acc_ref, scale, mask=None, first=False):
    factor = scale * LOG2E
    tiles = [slice(at, at + TILE) for at in range(0, q_ref.shape[2], TILE)]
    scores = [jnp.dot(keys, q_ref[seg, :, t], preferred_element_type=jnp.float32) for t in tiles]
    if mask is not None:
        scores = [jnp.where(mask, x, jnp.float32(-1e30)) for x in scores]
    tops = [jnp.max(x, axis=0, keepdims=True) for x in scores]
    if not first:
        before = [m_ref[seg, :, t] for t in tiles]
        tops = [jnp.maximum(b, x) for b, x in zip(before, tops)]
        shrinks = [jnp.exp2((b - x) * factor) for b, x in zip(before, tops)]
    probs = [jnp.exp2((x - top) * factor) for x, top in zip(scores, tops)]
    totals = [jnp.sum(p, axis=0, keepdims=True) for p in probs]
    sums = [
        lax.dot_general(
            values,
            p.astype(jnp.bfloat16),
            (((0,), (0,)), ((), ())),
            preferred_element_type=jnp.float32,
        )
        for p in probs
    ]
    if not first:
        totals = [n + l_ref[seg, :, t] * f for n, t, f in zip(totals, tiles, shrinks)]
        sums = [n + acc_ref[seg, :, t] * f for n, t, f in zip(sums, tiles, shrinks)]
    for t, top, total, summed in zip(tiles, tops, totals, sums):
        m_ref[seg, :, t] = top
        l_ref[seg, :, t] = total
        acc_ref[seg, :, t] = summed


def absorb_blocks(seg_ref, blocks_ref, q_ref, m_ref, l_ref, acc_ref, list_ref, count_ref, scale):
    places = seg_ref.shape[0]
    segs = q_ref.shape[0]
    head_dim = q_ref.shape[1]
    for seg in range(segs):
        count_ref[seg] = 0

    def place(at, carry):
        seg = seg_ref[at]

        @pl.when(seg >= 0)
        def _():
            used = count_ref[seg]
            list_ref[seg * places + used] = at
            count_ref[seg] = used + 1

        return carry

    lax.fori_loop(0, places, place, 0)

    def per_segment(seg, carry):
        count = count_ref[seg]

        def take(at, how_many):
            places_of = [list_ref[seg * places + at + i] for i in range(how_many)]
            found = [blocks_ref[p] for p in places_of]
            both = found[0] if how_many == 1 else jnp.concatenate(found, axis=0)
            absorb(seg, both[:, :head_dim], both[:, head_dim:], q_ref, m_ref, l_ref, acc_ref, scale)

        def quad(step, inner):
            take(4 * step, 4)
            return inner

        lax.fori_loop(0, count // 4, quad, 0)
        rest = count // 4 * 4

        @pl.when(count % 4 >= 2)
        def _():
            take(rest, 2)

        @pl.when(count % 2 == 1)
        def _():
            take(count - 1, 1)

        return carry

    lax.fori_loop(0, segs, per_segment, 0)


def own_kernel(scale, q_ref, own_ref, m_ref, l_ref, acc_ref):
    head_dim = q_ref.shape[1]
    seg_len = own_ref.shape[1]
    key_at = lax.broadcasted_iota(jnp.int32, (seg_len, TILE), 0)
    query_at = lax.broadcasted_iota(jnp.int32, (seg_len, TILE), 1) % seg_len
    causal = query_at >= key_at

    def own(seg, carry):
        keys, values = own_ref[seg, :, :head_dim], own_ref[seg, :, head_dim:]
        absorb(seg, keys, values, q_ref, m_ref, l_ref, acc_ref, scale, mask=causal, first=True)
        return carry

    lax.fori_loop(0, q_ref.shape[0], own, 0)


def carry_in(old, new):
    for source, target in zip(old, new):
        target[...] = source[...]


def chunk_kernel(scale, shared, seg_ref, q_ref, blocks_ref, m_in, l_in, acc_in, m_ref, l_ref, acc_ref, list_ref, count_ref):
    carry_in((m_in, l_in, acc_in), (m_ref, l_ref, acc_ref))
    absorb_blocks(seg_ref, blocks_ref, q_ref, m_ref, l_ref, acc_ref, list_ref, count_ref, scale)
    head_dim = q_ref.shape[1]

    def step(seg, carry):
        for at in range(0, len(shared), 4):
            found = jnp.concatenate([blocks_ref[p] for p in shared[at : at + 4]], axis=0)
            keys, values = found[:, :head_dim], found[:, head_dim:]
            absorb(seg, keys, values, q_ref, m_ref, l_ref, acc_ref, scale)
        return carry

    if shared:
        lax.fori_loop(0, q_ref.shape[0], step, 0)


def last_kernel(scale, seg_a_ref, seg_b_ref, x_ref, q_in, blocks_a_ref, blocks_b_ref, m_in, l_in, acc_in, *refs):
    outs, (q_ref, m_ref, l_ref, acc_ref, list_ref, count_ref, sems) = refs[:-7], refs[-7:]
    pairs = ((q_in, q_ref), (m_in, m_ref), (l_in, l_ref), (acc_in, acc_ref))
    copies = [pltpu.make_async_copy(a, b, sems.at[i]) for i, (a, b) in enumerate(pairs)]
    for copy in copies:
        copy.start()
    for copy in copies:
        copy.wait()
    for seg_ref, blocks_ref in ((seg_a_ref, blocks_a_ref), (seg_b_ref, blocks_b_ref)):
        absorb_blocks(
            seg_ref, blocks_ref, q_ref, m_ref, l_ref, acc_ref, list_ref, count_ref, scale
        )
    seg_len = outs[0].shape[0]
    head_dim = q_ref.shape[1]
    group = q_ref.shape[2] // seg_len
    segs = q_ref.shape[0]

    for step, out_ref in enumerate(outs):
        seg = (x_ref[0] + step) % segs
        for g in range(group):
            cols = slice(g * seg_len, (g + 1) * seg_len)
            value = acc_ref[seg, :, cols] / l_ref[seg, :, cols]
            out_ref[:, g * head_dim : (g + 1) * head_dim] = value.T.astype(jnp.bfloat16)


def pick_kernel(sources, n_in, rows_ref, *refs):
    count = len(sources)
    inputs, outputs = refs[:n_in], refs[n_in : n_in + count]
    buffers, reads, write = refs[n_in + count : n_in + 2 * count], refs[-1 - count : -1], refs[-1]
    base = 0
    for names, buffer, read in zip(sources, buffers, reads):

        def start(at, carry, names=names, buffer=buffer, read=read, base=base):
            for inner, name in enumerate(names):
                place = at * len(names) + inner
                block = inputs[name].at[rows_ref[base + place]]
                pltpu.make_async_copy(block, buffer.at[place], read.at[at]).start()
            return carry

        lax.fori_loop(0, buffer.shape[0] // len(names), start, 0)
        base += buffer.shape[0]
    for number, (names, buffer, out_ref, read) in enumerate(zip(sources, buffers, outputs, reads)):

        def pass_on(at, carry, names=names, buffer=buffer, out_ref=out_ref, read=read, number=number):
            part = pl.ds(at * len(names), len(names))
            pltpu.make_async_copy(buffer.at[part], buffer.at[part], read.at[at]).wait()
            pltpu.make_async_copy(buffer.at[part], out_ref.at[part], write.at[number]).start()
            return carry

        lax.fori_loop(0, buffer.shape[0] // len(names), pass_on, 0)
    for number, (buffer, out_ref) in enumerate(zip(buffers, outputs)):
        pltpu.make_async_copy(buffer, out_ref, write.at[number]).wait()


def column_tiles(columns):
    return [slice(at, at + PROJECT_TILE) for at in range(0, columns, PROJECT_TILE)]


def times(rows, weight):
    return jnp.dot(rows, weight, preferred_element_type=jnp.float32)


def stage_kernel(rows_ref, weight_ref, *refs):
    fetched, (total_ref, *staged), (own_ref, sems) = refs[:3], refs[3:7], refs[7:]
    pairs = [(weight_ref, own_ref)] + list(zip(fetched, staged))
    copies = [pltpu.make_async_copy(a, b, sems.at[i]) for i, (a, b) in enumerate(pairs)]
    for copy in copies:
        copy.start()
    copies[0].wait()
    for tile in column_tiles(total_ref.shape[1]):
        total_ref[:, tile] = times(rows_ref[...], own_ref[:, tile])
    for copy in copies[1:]:
        copy.wait()


def sides_kernel(c_ref, total_ref, right_ref, left_ref, mine_ref, other_ref, out_ref):
    right, left = right_ref[...], left_ref[...]
    even = c_ref[0] == 0
    first, second = jnp.where(even, right, left), jnp.where(even, left, right)
    for tile in column_tiles(out_ref.shape[1]):
        out_ref[:, tile] = (
            total_ref[:, tile] + times(first, mine_ref[:, tile]) + times(second, other_ref[:, tile])
        )


def far_kernel(total_ref, rows_ref, weight_ref, out_ref, buffer_ref, sems):
    copies = []
    for i, tile in enumerate(column_tiles(out_ref.shape[1])):
        total = total_ref[:, tile] + times(rows_ref[...], weight_ref[:, tile])
        buffer_ref[:, tile] = total.astype(out_ref.dtype)
        copies.append(
            pltpu.make_async_copy(buffer_ref.at[:, tile], out_ref.at[:, tile], sems.at[i])
        )
        copies[-1].start()
    for copy in copies:
        copy.wait()


VMEM = pl.BlockSpec(memory_space=pltpu.VMEM)
SMEM = pl.BlockSpec(memory_space=pltpu.SMEM)
ANY = pl.BlockSpec(memory_space=pl.ANY)
HBM = pl.BlockSpec(memory_space=pltpu.HBM)


def state_shapes(q):
    segs, head_dim, columns = q.shape
    return [
        jax.ShapeDtypeStruct((segs, 1, columns), jnp.float32),
        jax.ShapeDtypeStruct((segs, 1, columns), jnp.float32),
        jax.ShapeDtypeStruct((segs, head_dim, columns), jnp.float32),
    ]


def params():
    return pltpu.CompilerParams(vmem_limit_bytes=40 * 1024 * 1024)


def tables(places, segs):
    return [pltpu.SMEM((segs * places,), jnp.int32), pltpu.SMEM((segs,), jnp.int32)]


def attend_own(q, own, scale):
    return pl.pallas_call(
        functools.partial(own_kernel, scale),
        out_shape=state_shapes(q),
        in_specs=[VMEM, VMEM],
        out_specs=[VMEM] * 3,
        compiler_params=params(),
        cost_estimate=SMALL,
    )(q, own)


def attend_chunk(q, seg_of, blocks, state, scale, shared=()):
    return pl.pallas_call(
        functools.partial(chunk_kernel, scale, shared),
        out_shape=state_shapes(q),
        in_specs=[SMEM] + [VMEM] * 5,
        out_specs=[VMEM] * 3,
        scratch_shapes=tables(seg_of.shape[0], q.shape[0]),
        compiler_params=params(),
        cost_estimate=ATTEND,
    )(seg_of, q, blocks, *state)


def attend_last(q, fetched, state, x, scale):
    (seg_a, blocks_a), (seg_b, blocks_b) = fetched
    segs, head_dim, columns = q.shape
    seg_len = blocks_a.shape[1]
    group = columns // seg_len
    places = max(seg_a.shape[0], seg_b.shape[0])
    return pl.pallas_call(
        functools.partial(last_kernel, scale),
        out_shape=[jax.ShapeDtypeStruct((seg_len, group * head_dim), jnp.bfloat16)] * segs,
        in_specs=[SMEM] * 3 + [HBM] + [VMEM] * 2 + [HBM] * 3,
        out_specs=[VMEM] * segs,
        scratch_shapes=[pltpu.VMEM(s.shape, s.dtype) for s in [q] + state_shapes(q)]
        + tables(places, segs)
        + [pltpu.SemaphoreType.DMA((4,))],
        compiler_params=small_params(56),
        cost_estimate=ATTEND,
    )(seg_a, seg_b, x, q, blocks_a, blocks_b, *state)


def pick(plan, buffers, told=None):
    block, dtype = buffers[0].shape[1:], buffers[0].dtype
    names = tuple(n for n, _ in plan)
    sizes = [rows.size for _, rows in plan]
    out = pl.pallas_call(
        functools.partial(pick_kernel, names, len(buffers)),
        out_shape=[jax.ShapeDtypeStruct((size,) + block, dtype) for size in sizes],
        in_specs=[SMEM] + [ANY] * len(buffers),
        out_specs=[ANY] * len(plan),
        scratch_shapes=[pltpu.VMEM((size,) + block, dtype) for size in sizes]
        + [pltpu.SemaphoreType.DMA((size // len(n),)) for n, size in zip(names, sizes)]
        + [pltpu.SemaphoreType.DMA((len(plan),))],
        compiler_params=pltpu.CompilerParams(vmem_limit_bytes=56 * 1024 * 1024),
        cost_estimate=told or SMALL,
    )(jnp.concatenate([rows.reshape(-1) for _, rows in plan]), *buffers)
    return [x.reshape(rows.shape + block) for x, (_, rows) in zip(out, plan)]


def small_params(mebibytes):
    return pltpu.CompilerParams(vmem_limit_bytes=mebibytes * 1024 * 1024)


def stage(rows, own, fetched):
    total = jax.ShapeDtypeStruct((rows.shape[0], own.shape[1]), jnp.float32)
    return pl.pallas_call(
        stage_kernel,
        out_shape=[total] + [jax.ShapeDtypeStruct(w.shape, w.dtype) for w in fetched],
        in_specs=[VMEM] + [ANY] * 4,
        out_specs=[VMEM] * 4,
        scratch_shapes=[pltpu.VMEM(own.shape, own.dtype), pltpu.SemaphoreType.DMA((4,))],
        compiler_params=small_params(30),
        cost_estimate=SMALL,
    )(rows, own, *fetched)


def add_sides(c, total, right, left, mine, other):
    return pl.pallas_call(
        sides_kernel,
        out_shape=jax.ShapeDtypeStruct(total.shape, total.dtype),
        in_specs=[SMEM] + [VMEM] * 5,
        out_specs=VMEM,
        compiler_params=small_params(8),
        cost_estimate=SMALL,
    )(c, total, right, left, mine, other)


def add_far(total, rows, weight):
    return pl.pallas_call(
        far_kernel,
        out_shape=jax.ShapeDtypeStruct(total.shape, jnp.bfloat16),
        in_specs=[VMEM] * 3,
        out_specs=ANY,
        scratch_shapes=[
            pltpu.VMEM(total.shape, jnp.bfloat16),
            pltpu.SemaphoreType.DMA((total.shape[1] // PROJECT_TILE,)),
        ],
        compiler_params=small_params(8),
        cost_estimate=SMALL,
    )(total, rows, weight)


def together(*arrays):
    return lax.optimization_barrier(arrays)


def per_device(queries, new_kv, prompt_kv, pool, parents, lengths, location, out_weight):
    tok_rows = queries.shape[0]
    seg_dev, max_anc = parents.shape
    head_dim = prompt_kv.shape[1] // 2
    group = queries.shape[1] // head_dim
    seg_len = tok_rows // seg_dev
    blocks = pool.shape[0]
    scale = head_dim ** (-0.5)
    n_leaf = lax.axis_size("leaf")
    n_head = lax.axis_size("head")
    planes = n_leaf // LANES
    capacity = 2
    me = lax.axis_index("leaf")
    plane = me // LANES
    core = me % CORES

    def along_z(x, step):
        pairs = [(d, (d + step * LANES) % n_leaf) for d in range(n_leaf)]
        return lax.ppermute(x, "leaf", pairs)

    def along_x(x, step):
        return lax.ppermute(x, "head", [(d, (d + step) % n_head) for d in range(n_head)])

    def other_core(x):
        return lax.ppermute(x, "leaf", [(d, d ^ 1) for d in range(n_leaf)])

    in_plane = [[p * LANES + lane for lane in range(LANES)] for p in range(planes)]

    def spread(x):
        return lax.all_to_all(x, "leaf", 0, 0, tiled=True, axis_index_groups=in_plane)

    up1 = along_z(pool, 1)
    down1 = along_z(pool, -1)

    n_all = n_leaf * n_head

    def by_core(x):
        pairs = []
        for d in range(n_all):
            leaf, head = divmod(d, n_head)
            step = -1 if leaf % CORES == 0 else 1
            pairs.append((d, leaf * n_head + (head + step) % n_head))
        return lax.ppermute(x, ("leaf", "head"), pairs)

    weight1 = by_core(out_weight)

    slots = seg_dev * max_anc
    stored = location[parents].reshape(-1)
    live = (jnp.arange(max_anc)[None, :] < lengths[:, None]).reshape(-1)
    owner = jnp.where(live, stored // blocks, -1)
    row = stored % blocks
    order = jnp.arange(slots)
    rank = jnp.sum(
        (owner[:, None] == owner[None, :]) & (order[:, None] > order[None, :]), axis=1
    )
    dist = (plane - owner // LANES) % planes
    cell = jnp.where(live, (dist * LANES + owner % LANES) * capacity + rank, -1)
    hit = cell[None, :] == jnp.arange(n_leaf * capacity)[:, None]
    wanted = jnp.sum(jnp.where(hit, row[None, :], 0), axis=1).astype(jnp.int32)
    seg_of = jnp.sum(jnp.where(hit, (order // max_anc + 1)[None, :], 0), axis=1) - 1
    seg_of = seg_of.astype(jnp.int32).reshape(planes, LANES, capacity)
    per_lane = jnp.transpose(wanted.reshape(planes, LANES, capacity), (1, 0, 2))
    here = spread(per_lane.reshape(LANES, 1, planes * capacity))
    here = here.reshape(LANES, planes, capacity)

    q = jnp.transpose(
        queries.reshape(seg_dev, seg_len, group, head_dim), (0, 3, 2, 1)
    ).reshape(seg_dev, head_dim, group * seg_len)
    own = new_kv.reshape(seg_dev, seg_len, 2 * head_dim)
    state = attend_own(q, own, scale)
    here, *state = together(here, *state)

    def segs_at(dists, more=0):
        parts = [seg_of[d] for d in dists] + [jnp.full((LANES, more), -1, jnp.int32)] * bool(more)
        return jnp.concatenate(parts, axis=1).reshape(-1)

    def flat(x):
        return x.reshape((-1,) + x.shape[-2:])

    prompt_rows, width = prompt_kv.shape
    table = here.reshape(1, -1).astype(prompt_kv.dtype)
    table = jnp.pad(table, ((0, prompt_rows - 1), (0, width - table.shape[1])))
    notice = jnp.concatenate([prompt_kv, table], axis=0)
    same_lane = [[p * LANES + lane for p in range(planes)] for lane in range(LANES)]
    notices = lax.all_to_all(
        jnp.broadcast_to(notice[None], (planes,) + notice.shape),
        "leaf",
        0,
        0,
        tiled=True,
        axis_index_groups=same_lane,
    )
    notices, up1, down1 = together(notices, up1, down1)
    up2 = along_z(up1, 1)
    down2 = along_z(down1, -1)
    lane_prompt = notices[:, :prompt_rows].reshape(1, planes * prompt_rows, width)
    asked = notices[:, prompt_rows, : LANES * planes * capacity].astype(jnp.int32)
    asked = asked.reshape(planes, LANES, planes, capacity)
    asked = lax.dynamic_slice_in_dim(jnp.concatenate([asked, asked], axis=0), plane, planes, 0)

    zero = jnp.zeros((LANES, 1), jnp.int32)
    rows01 = jnp.concatenate([here[:, 0], here[:, 1], here[:, planes - 1], zero], axis=1)
    plan01 = ((0, 0, 1, 1, 2, 2, 3), rows01)
    got01 = spread(pick([plan01], [pool, up1, down1, lane_prompt])[0])
    up2, down2, weight1 = together(up2, down2, weight1)
    weight2 = by_core(weight1)
    ask_up = asked[1, :, 3]
    ask_down = asked[planes - 1, :, planes - 3]
    on_core = (jnp.arange(LANES) % CORES)[:, None]
    ask_far = jnp.where(on_core == 0, asked[2, :, 4], asked[planes - 2, :, 4])
    rows2 = jnp.concatenate([here[:, 2], here[:, planes - 2], ask_far], axis=1)
    send_up, send_down, rest = pick(
        [
            ((0, 0), ask_up),
            ((1, 1), ask_down),
            ((0, 0, 1, 1, 0, 0, 0, 0, 1, 1, 1, 1), rows2),
        ],
        [up2, down2],
        LARGE,
    )
    up3 = along_z(send_up, 1)
    down3 = along_z(send_down, -1)
    rest, got01 = together(rest, got01)
    got2 = spread(rest)
    weight1_too = other_core(weight1)
    every = 3 * capacity + 1
    prompts = tuple(range(every - 1, LANES * every, every))
    state = attend_chunk(
        q, segs_at([0, 1, planes - 1], 1), flat(got01), state, scale, shared=prompts
    )

    up3, down3, *state = together(up3, down3, *state)
    reach = [(d, (d + (2 if d % CORES == 0 else -2) * LANES) % n_leaf) for d in range(n_leaf)]
    got4 = lax.ppermute(got2[:, 2 * capacity :], "leaf", reach)
    got3 = spread(jnp.concatenate([up3, down3], axis=1))
    state = attend_chunk(q, segs_at([2, planes - 2], capacity), flat(got2), state, scale)

    got3, got4, weight1_too, *state = together(got3, got4, weight1_too, *state)
    x = lax.axis_index("head").astype(jnp.int32).reshape(1)
    fetched = ((segs_at([3, planes - 3]), flat(got3)), (segs_at([4]), flat(got4)))
    keep, to_up, to_far, to_down = attend_last(q, fetched, state, x, scale)

    from_far = along_x(to_far, 2)
    from_down = along_x(to_up, 1)
    from_up = along_x(to_down, -1)
    c = core.astype(jnp.int32).reshape(1)
    total, mine, other, far = stage(keep, out_weight, (weight1, weight1_too, weight2))
    total = add_sides(c, total, from_up, from_down, mine, other)
    return add_far(total, from_far, far)


def solution(mesh):
    return jax.shard_map(
        per_device,
        mesh=mesh,
        in_specs=(
            P("leaf", "head"),
            P("leaf", "head"),
            P("leaf", "head"),
            P("leaf", None, "head"),
            P("leaf", None),
            P("leaf"),
            P(),
            P("head", None),
        ),
        out_specs=P(("leaf", "head"), None),
        check_vma=False,
    )
```

```python
import functools

import jax
import jax.numpy as jnp
from jax import lax
from jax.experimental import pallas as pl
from jax.experimental.pallas import tpu as pltpu
from jax.sharding import PartitionSpec as P

Y_SIZE = 4
CORES = 2
LANES = Y_SIZE * CORES
LOG2E = 1.4426950408889634
TILE = 256
PROJECT_TILE = 1024
SMALL = pl.CostEstimate(flops=1 << 16, bytes_accessed=1 << 16, transcendentals=0)
ATTEND = pl.CostEstimate(flops=1 << 35, bytes_accessed=1 << 16, transcendentals=0)
LARGE = pl.CostEstimate(flops=1 << 35, bytes_accessed=1 << 16, transcendentals=0)


def absorb(seg, keys, values, q_ref, m_ref, l_ref, acc_ref, scale, mask=None, first=False):
    factor = scale * LOG2E
    tiles = [slice(at, at + TILE) for at in range(0, q_ref.shape[2], TILE)]
    scores = [jnp.dot(keys, q_ref[seg, :, t], preferred_element_type=jnp.float32) for t in tiles]
    if mask is not None:
        scores = [jnp.where(mask, x, jnp.float32(-1e30)) for x in scores]
    tops = [jnp.max(x, axis=0, keepdims=True) for x in scores]
    if not first:
        before = [m_ref[seg, :, t] for t in tiles]
        tops = [jnp.maximum(b, x) for b, x in zip(before, tops)]
        shrinks = [jnp.exp2((b - x) * factor) for b, x in zip(before, tops)]
    probs = [jnp.exp2((x - top) * factor) for x, top in zip(scores, tops)]
    totals = [jnp.sum(p, axis=0, keepdims=True) for p in probs]
    sums = [
        lax.dot_general(
            values,
            p.astype(jnp.bfloat16),
            (((0,), (0,)), ((), ())),
            preferred_element_type=jnp.float32,
        )
        for p in probs
    ]
    if not first:
        totals = [n + l_ref[seg, :, t] * f for n, t, f in zip(totals, tiles, shrinks)]
        sums = [n + acc_ref[seg, :, t] * f for n, t, f in zip(sums, tiles, shrinks)]
    for t, top, total, summed in zip(tiles, tops, totals, sums):
        m_ref[seg, :, t] = top
        l_ref[seg, :, t] = total
        acc_ref[seg, :, t] = summed


def absorb_blocks(seg_ref, blocks_ref, q_ref, m_ref, l_ref, acc_ref, list_ref, count_ref, scale):
    places = seg_ref.shape[0]
    segs = q_ref.shape[0]
    head_dim = q_ref.shape[1]
    for seg in range(segs):
        count_ref[seg] = 0

    def place(at, carry):
        seg = seg_ref[at]

        @pl.when(seg >= 0)
        def _():
            used = count_ref[seg]
            list_ref[seg * places + used] = at
            count_ref[seg] = used + 1

        return carry

    lax.fori_loop(0, places, place, 0)

    def per_segment(seg, carry):
        count = count_ref[seg]

        def take(at, how_many):
            places_of = [list_ref[seg * places + at + i] for i in range(how_many)]
            found = [blocks_ref[p] for p in places_of]
            both = found[0] if how_many == 1 else jnp.concatenate(found, axis=0)
            absorb(seg, both[:, :head_dim], both[:, head_dim:], q_ref, m_ref, l_ref, acc_ref, scale)

        def quad(step, inner):
            take(4 * step, 4)
            return inner

        lax.fori_loop(0, count // 4, quad, 0)
        rest = count // 4 * 4

        @pl.when(count % 4 >= 2)
        def _():
            take(rest, 2)

        @pl.when(count % 2 == 1)
        def _():
            take(count - 1, 1)

        return carry

    lax.fori_loop(0, segs, per_segment, 0)


def own_kernel(scale, q_ref, own_ref, m_ref, l_ref, acc_ref):
    head_dim = q_ref.shape[1]
    seg_len = own_ref.shape[1]
    key_at = lax.broadcasted_iota(jnp.int32, (seg_len, TILE), 0)
    query_at = lax.broadcasted_iota(jnp.int32, (seg_len, TILE), 1) % seg_len
    causal = query_at >= key_at

    def own(seg, carry):
        keys, values = own_ref[seg, :, :head_dim], own_ref[seg, :, head_dim:]
        absorb(seg, keys, values, q_ref, m_ref, l_ref, acc_ref, scale, mask=causal, first=True)
        return carry

    lax.fori_loop(0, q_ref.shape[0], own, 0)


def carry_in(old, new):
    for source, target in zip(old, new):
        target[...] = source[...]


def chunk_kernel(scale, shared, seg_ref, q_ref, blocks_ref, m_in, l_in, acc_in, m_ref, l_ref, acc_ref, list_ref, count_ref):
    carry_in((m_in, l_in, acc_in), (m_ref, l_ref, acc_ref))
    absorb_blocks(seg_ref, blocks_ref, q_ref, m_ref, l_ref, acc_ref, list_ref, count_ref, scale)
    head_dim = q_ref.shape[1]

    def step(seg, carry):
        for at in range(0, len(shared), 4):
            found = jnp.concatenate([blocks_ref[p] for p in shared[at : at + 4]], axis=0)
            keys, values = found[:, :head_dim], found[:, head_dim:]
            absorb(seg, keys, values, q_ref, m_ref, l_ref, acc_ref, scale)
        return carry

    if shared:
        lax.fori_loop(0, q_ref.shape[0], step, 0)


def last_kernel(scale, seg_a_ref, seg_b_ref, x_ref, q_ref, blocks_a_ref, blocks_b_ref, m_in, l_in, acc_in, *refs):
    outs, (m_ref, l_ref, acc_ref, list_ref, count_ref) = refs[:-5], refs[-5:]
    carry_in((m_in, l_in, acc_in), (m_ref, l_ref, acc_ref))
    for seg_ref, blocks_ref in ((seg_a_ref, blocks_a_ref), (seg_b_ref, blocks_b_ref)):
        absorb_blocks(
            seg_ref, blocks_ref, q_ref, m_ref, l_ref, acc_ref, list_ref, count_ref, scale
        )
    seg_len = outs[0].shape[0]
    head_dim = q_ref.shape[1]
    group = q_ref.shape[2] // seg_len
    segs = q_ref.shape[0]

    for step, out_ref in enumerate(outs):
        seg = (x_ref[0] + step) % segs
        for g in range(group):
            cols = slice(g * seg_len, (g + 1) * seg_len)
            value = acc_ref[seg, :, cols] / l_ref[seg, :, cols]
            out_ref[:, g * head_dim : (g + 1) * head_dim] = value.T.astype(jnp.bfloat16)


def pick_kernel(sources, n_in, rows_ref, *refs):
    count = len(sources)
    inputs, outputs = refs[:n_in], refs[n_in : n_in + count]
    buffers, reads, write = refs[n_in + count : n_in + 2 * count], refs[-1 - count : -1], refs[-1]
    base = 0
    for names, buffer, read in zip(sources, buffers, reads):

        def start(at, carry, names=names, buffer=buffer, read=read, base=base):
            for inner, name in enumerate(names):
                place = at * len(names) + inner
                block = inputs[name].at[rows_ref[base + place]]
                pltpu.make_async_copy(block, buffer.at[place], read.at[at]).start()
            return carry

        lax.fori_loop(0, buffer.shape[0] // len(names), start, 0)
        base += buffer.shape[0]
    for number, (names, buffer, out_ref, read) in enumerate(zip(sources, buffers, outputs, reads)):

        def pass_on(at, carry, names=names, buffer=buffer, out_ref=out_ref, read=read, number=number):
            part = pl.ds(at * len(names), len(names))
            pltpu.make_async_copy(buffer.at[part], buffer.at[part], read.at[at]).wait()
            pltpu.make_async_copy(buffer.at[part], out_ref.at[part], write.at[number]).start()
            return carry

        lax.fori_loop(0, buffer.shape[0] // len(names), pass_on, 0)
    for number, (buffer, out_ref) in enumerate(zip(buffers, outputs)):
        pltpu.make_async_copy(buffer, out_ref, write.at[number]).wait()


def column_tiles(columns):
    return [slice(at, at + PROJECT_TILE) for at in range(0, columns, PROJECT_TILE)]


def times(rows, weight):
    return jnp.dot(rows, weight, preferred_element_type=jnp.float32)


def stage_kernel(rows_ref, weight_ref, *refs):
    fetched, (total_ref, *staged), (own_ref, sems) = refs[:3], refs[3:7], refs[7:]
    pairs = [(weight_ref, own_ref)] + list(zip(fetched, staged))
    copies = [pltpu.make_async_copy(a, b, sems.at[i]) for i, (a, b) in enumerate(pairs)]
    for copy in copies:
        copy.start()
    copies[0].wait()
    for tile in column_tiles(total_ref.shape[1]):
        total_ref[:, tile] = times(rows_ref[...], own_ref[:, tile])
    for copy in copies[1:]:
        copy.wait()


def sides_kernel(c_ref, total_ref, right_ref, left_ref, mine_ref, other_ref, out_ref):
    right, left = right_ref[...], left_ref[...]
    even = c_ref[0] == 0
    first, second = jnp.where(even, right, left), jnp.where(even, left, right)
    for tile in column_tiles(out_ref.shape[1]):
        out_ref[:, tile] = (
            total_ref[:, tile] + times(first, mine_ref[:, tile]) + times(second, other_ref[:, tile])
        )


def far_kernel(total_ref, rows_ref, weight_ref, out_ref, buffer_ref, sems):
    copies = []
    for i, tile in enumerate(column_tiles(out_ref.shape[1])):
        total = total_ref[:, tile] + times(rows_ref[...], weight_ref[:, tile])
        buffer_ref[:, tile] = total.astype(out_ref.dtype)
        copies.append(
            pltpu.make_async_copy(buffer_ref.at[:, tile], out_ref.at[:, tile], sems.at[i])
        )
        copies[-1].start()
    for copy in copies:
        copy.wait()


VMEM = pl.BlockSpec(memory_space=pltpu.VMEM)
SMEM = pl.BlockSpec(memory_space=pltpu.SMEM)
ANY = pl.BlockSpec(memory_space=pl.ANY)


def state_shapes(q):
    segs, head_dim, columns = q.shape
    return [
        jax.ShapeDtypeStruct((segs, 1, columns), jnp.float32),
        jax.ShapeDtypeStruct((segs, 1, columns), jnp.float32),
        jax.ShapeDtypeStruct((segs, head_dim, columns), jnp.float32),
    ]


def params():
    return pltpu.CompilerParams(vmem_limit_bytes=40 * 1024 * 1024)


def tables(places, segs):
    return [pltpu.SMEM((segs * places,), jnp.int32), pltpu.SMEM((segs,), jnp.int32)]


def attend_own(q, own, scale):
    return pl.pallas_call(
        functools.partial(own_kernel, scale),
        out_shape=state_shapes(q),
        in_specs=[VMEM, VMEM],
        out_specs=[VMEM] * 3,
        compiler_params=params(),
        cost_estimate=SMALL,
    )(q, own)


def attend_chunk(q, seg_of, blocks, state, scale, shared=()):
    return pl.pallas_call(
        functools.partial(chunk_kernel, scale, shared),
        out_shape=state_shapes(q),
        in_specs=[SMEM] + [VMEM] * 5,
        out_specs=[VMEM] * 3,
        scratch_shapes=tables(seg_of.shape[0], q.shape[0]),
        compiler_params=params(),
        cost_estimate=ATTEND,
    )(seg_of, q, blocks, *state)


def attend_last(q, fetched, state, x, scale):
    (seg_a, blocks_a), (seg_b, blocks_b) = fetched
    segs, head_dim, columns = q.shape
    seg_len = blocks_a.shape[1]
    group = columns // seg_len
    places = max(seg_a.shape[0], seg_b.shape[0])
    return pl.pallas_call(
        functools.partial(last_kernel, scale),
        out_shape=[jax.ShapeDtypeStruct((seg_len, group * head_dim), jnp.bfloat16)] * segs,
        in_specs=[SMEM] * 3 + [VMEM] * 6,
        out_specs=[VMEM] * segs,
        scratch_shapes=[pltpu.VMEM(s.shape, s.dtype) for s in state_shapes(q)]
        + tables(places, segs),
        compiler_params=params(),
        cost_estimate=ATTEND,
    )(seg_a, seg_b, x, q, blocks_a, blocks_b, *state)


def pick(plan, buffers, told=None):
    block, dtype = buffers[0].shape[1:], buffers[0].dtype
    names = tuple(n for n, _ in plan)
    sizes = [rows.size for _, rows in plan]
    out = pl.pallas_call(
        functools.partial(pick_kernel, names, len(buffers)),
        out_shape=[jax.ShapeDtypeStruct((size,) + block, dtype) for size in sizes],
        in_specs=[SMEM] + [ANY] * len(buffers),
        out_specs=[ANY] * len(plan),
        scratch_shapes=[pltpu.VMEM((size,) + block, dtype) for size in sizes]
        + [pltpu.SemaphoreType.DMA((size // len(n),)) for n, size in zip(names, sizes)]
        + [pltpu.SemaphoreType.DMA((len(plan),))],
        compiler_params=pltpu.CompilerParams(vmem_limit_bytes=56 * 1024 * 1024),
        cost_estimate=told or SMALL,
    )(jnp.concatenate([rows.reshape(-1) for _, rows in plan]), *buffers)
    return [x.reshape(rows.shape + block) for x, (_, rows) in zip(out, plan)]


def small_params(mebibytes):
    return pltpu.CompilerParams(vmem_limit_bytes=mebibytes * 1024 * 1024)


def stage(rows, own, fetched):
    total = jax.ShapeDtypeStruct((rows.shape[0], own.shape[1]), jnp.float32)
    return pl.pallas_call(
        stage_kernel,
        out_shape=[total] + [jax.ShapeDtypeStruct(w.shape, w.dtype) for w in fetched],
        in_specs=[VMEM] + [ANY] * 4,
        out_specs=[VMEM] * 4,
        scratch_shapes=[pltpu.VMEM(own.shape, own.dtype), pltpu.SemaphoreType.DMA((4,))],
        compiler_params=small_params(30),
        cost_estimate=SMALL,
    )(rows, own, *fetched)


def add_sides(c, total, right, left, mine, other):
    return pl.pallas_call(
        sides_kernel,
        out_shape=jax.ShapeDtypeStruct(total.shape, total.dtype),
        in_specs=[SMEM] + [VMEM] * 5,
        out_specs=VMEM,
        compiler_params=small_params(8),
        cost_estimate=SMALL,
    )(c, total, right, left, mine, other)


def add_far(total, rows, weight):
    return pl.pallas_call(
        far_kernel,
        out_shape=jax.ShapeDtypeStruct(total.shape, jnp.bfloat16),
        in_specs=[VMEM] * 3,
        out_specs=ANY,
        scratch_shapes=[
            pltpu.VMEM(total.shape, jnp.bfloat16),
            pltpu.SemaphoreType.DMA((total.shape[1] // PROJECT_TILE,)),
        ],
        compiler_params=small_params(8),
        cost_estimate=SMALL,
    )(total, rows, weight)


def together(*arrays):
    return lax.optimization_barrier(arrays)


def per_device(queries, new_kv, prompt_kv, pool, parents, lengths, location, out_weight):
    tok_rows = queries.shape[0]
    seg_dev, max_anc = parents.shape
    head_dim = prompt_kv.shape[1] // 2
    group = queries.shape[1] // head_dim
    seg_len = tok_rows // seg_dev
    blocks = pool.shape[0]
    scale = head_dim ** (-0.5)
    n_leaf = lax.axis_size("leaf")
    n_head = lax.axis_size("head")
    planes = n_leaf // LANES
    capacity = 2
    me = lax.axis_index("leaf")
    plane = me // LANES
    core = me % CORES

    def along_z(x, step):
        pairs = [(d, (d + step * LANES) % n_leaf) for d in range(n_leaf)]
        return lax.ppermute(x, "leaf", pairs)

    def along_x(x, step):
        return lax.ppermute(x, "head", [(d, (d + step) % n_head) for d in range(n_head)])

    def other_core(x):
        return lax.ppermute(x, "leaf", [(d, d ^ 1) for d in range(n_leaf)])

    in_plane = [[p * LANES + lane for lane in range(LANES)] for p in range(planes)]

    def spread(x):
        return lax.all_to_all(x, "leaf", 0, 0, tiled=True, axis_index_groups=in_plane)

    up1 = along_z(pool, 1)
    down1 = along_z(pool, -1)

    n_all = n_leaf * n_head

    def by_core(x):
        pairs = []
        for d in range(n_all):
            leaf, head = divmod(d, n_head)
            step = -1 if leaf % CORES == 0 else 1
            pairs.append((d, leaf * n_head + (head + step) % n_head))
        return lax.ppermute(x, ("leaf", "head"), pairs)

    weight1 = by_core(out_weight)

    slots = seg_dev * max_anc
    stored = location[parents].reshape(-1)
    live = (jnp.arange(max_anc)[None, :] < lengths[:, None]).reshape(-1)
    owner = jnp.where(live, stored // blocks, -1)
    row = stored % blocks
    order = jnp.arange(slots)
    rank = jnp.sum(
        (owner[:, None] == owner[None, :]) & (order[:, None] > order[None, :]), axis=1
    )
    dist = (plane - owner // LANES) % planes
    cell = jnp.where(live, (dist * LANES + owner % LANES) * capacity + rank, -1)
    hit = cell[None, :] == jnp.arange(n_leaf * capacity)[:, None]
    wanted = jnp.sum(jnp.where(hit, row[None, :], 0), axis=1).astype(jnp.int32)
    seg_of = jnp.sum(jnp.where(hit, (order // max_anc + 1)[None, :], 0), axis=1) - 1
    seg_of = seg_of.astype(jnp.int32).reshape(planes, LANES, capacity)
    per_lane = jnp.transpose(wanted.reshape(planes, LANES, capacity), (1, 0, 2))
    here = spread(per_lane.reshape(LANES, 1, planes * capacity))
    here = here.reshape(LANES, planes, capacity)

    q = jnp.transpose(
        queries.reshape(seg_dev, seg_len, group, head_dim), (0, 3, 2, 1)
    ).reshape(seg_dev, head_dim, group * seg_len)
    own = new_kv.reshape(seg_dev, seg_len, 2 * head_dim)
    state = attend_own(q, own, scale)
    here, *state = together(here, *state)

    def segs_at(dists, more=0):
        parts = [seg_of[d] for d in dists] + [jnp.full((LANES, more), -1, jnp.int32)] * bool(more)
        return jnp.concatenate(parts, axis=1).reshape(-1)

    def flat(x):
        return x.reshape((-1,) + x.shape[-2:])

    prompt_rows, width = prompt_kv.shape
    table = here.reshape(1, -1).astype(prompt_kv.dtype)
    table = jnp.pad(table, ((0, prompt_rows - 1), (0, width - table.shape[1])))
    notice = jnp.concatenate([prompt_kv, table], axis=0)
    same_lane = [[p * LANES + lane for p in range(planes)] for lane in range(LANES)]
    notices = lax.all_to_all(
        jnp.broadcast_to(notice[None], (planes,) + notice.shape),
        "leaf",
        0,
        0,
        tiled=True,
        axis_index_groups=same_lane,
    )
    notices, up1, down1 = together(notices, up1, down1)
    up2 = along_z(up1, 1)
    down2 = along_z(down1, -1)
    lane_prompt = notices[:, :prompt_rows].reshape(1, planes * prompt_rows, width)
    asked = notices[:, prompt_rows, : LANES * planes * capacity].astype(jnp.int32)
    asked = asked.reshape(planes, LANES, planes, capacity)
    asked = lax.dynamic_slice_in_dim(jnp.concatenate([asked, asked], axis=0), plane, planes, 0)

    zero = jnp.zeros((LANES, 1), jnp.int32)
    rows01 = jnp.concatenate([here[:, 0], here[:, 1], here[:, planes - 1], zero], axis=1)
    plan01 = ((0, 0, 1, 1, 2, 2, 3), rows01)
    got01 = spread(pick([plan01], [pool, up1, down1, lane_prompt])[0])
    up2, down2, weight1 = together(up2, down2, weight1)
    weight2 = by_core(weight1)
    ask_up = asked[1, :, 3]
    ask_down = asked[planes - 1, :, planes - 3]
    on_core = (jnp.arange(LANES) % CORES)[:, None]
    ask_far = jnp.where(on_core == 0, asked[2, :, 4], asked[planes - 2, :, 4])
    rows2 = jnp.concatenate([here[:, 2], here[:, planes - 2], ask_far], axis=1)
    send_up, send_down, rest = pick(
        [
            ((0, 0), ask_up),
            ((1, 1), ask_down),
            ((0, 0, 1, 1, 0, 0, 0, 0, 1, 1, 1, 1), rows2),
        ],
        [up2, down2],
        LARGE,
    )
    up3 = along_z(send_up, 1)
    down3 = along_z(send_down, -1)
    rest, got01 = together(rest, got01)
    got2 = spread(rest)
    weight1_too = other_core(weight1)
    every = 3 * capacity + 1
    prompts = tuple(range(every - 1, LANES * every, every))
    state = attend_chunk(
        q, segs_at([0, 1, planes - 1], 1), flat(got01), state, scale, shared=prompts
    )

    up3, down3, *state = together(up3, down3, *state)
    reach = [(d, (d + (2 if d % CORES == 0 else -2) * LANES) % n_leaf) for d in range(n_leaf)]
    got4 = lax.ppermute(got2[:, 2 * capacity :], "leaf", reach)
    got3 = spread(jnp.concatenate([up3, down3], axis=1))
    state = attend_chunk(q, segs_at([2, planes - 2], capacity), flat(got2), state, scale)

    got3, got4, weight1_too, *state = together(got3, got4, weight1_too, *state)
    x = lax.axis_index("head").astype(jnp.int32).reshape(1)
    fetched = ((segs_at([3, planes - 3]), flat(got3)), (segs_at([4]), flat(got4)))
    keep, to_up, to_far, to_down = attend_last(q, fetched, state, x, scale)

    from_far = along_x(to_far, 2)
    from_down = along_x(to_up, 1)
    from_up = along_x(to_down, -1)
    c = core.astype(jnp.int32).reshape(1)
    total, mine, other, far = stage(keep, out_weight, (weight1, weight1_too, weight2))
    total = add_sides(c, total, from_up, from_down, mine, other)
    return add_far(total, from_far, far)


def solution(mesh):
    return jax.shard_map(
        per_device,
        mesh=mesh,
        in_specs=(
            P("leaf", "head"),
            P("leaf", "head"),
            P("leaf", "head"),
            P("leaf", None, "head"),
            P("leaf", None),
            P("leaf"),
            P(),
            P("head", None),
        ),
        out_specs=P(("leaf", "head"), None),
        check_vma=False,
    )
```

```python
import functools

import jax
import jax.numpy as jnp
from jax import lax
from jax.experimental import pallas as pl
from jax.experimental.pallas import tpu as pltpu
from jax.sharding import PartitionSpec as P

Y_SIZE = 4
CORES = 2
LANES = Y_SIZE * CORES
LOG2E = 1.4426950408889634
TILE = 256
PROJECT_TILE = 1024
SMALL = pl.CostEstimate(flops=1 << 16, bytes_accessed=1 << 16, transcendentals=0)
ATTEND = pl.CostEstimate(flops=1 << 35, bytes_accessed=1 << 16, transcendentals=0)
LARGE = pl.CostEstimate(flops=1 << 35, bytes_accessed=1 << 16, transcendentals=0)


def absorb(seg, keys, values, q_ref, m_ref, l_ref, acc_ref, scale, mask=None, first=False):
    factor = scale * LOG2E
    tiles = [slice(at, at + TILE) for at in range(0, q_ref.shape[2], TILE)]
    scores = [jnp.dot(keys, q_ref[seg, :, t], preferred_element_type=jnp.float32) for t in tiles]
    if mask is not None:
        scores = [jnp.where(mask, x, jnp.float32(-1e30)) for x in scores]
    tops = [jnp.max(x, axis=0, keepdims=True) for x in scores]
    if not first:
        before = [m_ref[seg, :, t] for t in tiles]
        tops = [jnp.maximum(b, x) for b, x in zip(before, tops)]
        shrinks = [jnp.exp2((b - x) * factor) for b, x in zip(before, tops)]
    probs = [jnp.exp2((x - top) * factor) for x, top in zip(scores, tops)]
    totals = [jnp.sum(p, axis=0, keepdims=True) for p in probs]
    sums = [
        lax.dot_general(
            values,
            p.astype(jnp.bfloat16),
            (((0,), (0,)), ((), ())),
            preferred_element_type=jnp.float32,
        )
        for p in probs
    ]
    if not first:
        totals = [n + l_ref[seg, :, t] * f for n, t, f in zip(totals, tiles, shrinks)]
        sums = [n + acc_ref[seg, :, t] * f for n, t, f in zip(sums, tiles, shrinks)]
    for t, top, total, summed in zip(tiles, tops, totals, sums):
        m_ref[seg, :, t] = top
        l_ref[seg, :, t] = total
        acc_ref[seg, :, t] = summed


def absorb_blocks(seg_ref, blocks_ref, q_ref, m_ref, l_ref, acc_ref, list_ref, count_ref, scale):
    places = seg_ref.shape[0]
    segs = q_ref.shape[0]
    head_dim = q_ref.shape[1]
    for seg in range(segs):
        count_ref[seg] = 0

    def place(at, carry):
        seg = seg_ref[at]

        @pl.when(seg >= 0)
        def _():
            used = count_ref[seg]
            list_ref[seg * places + used] = at
            count_ref[seg] = used + 1

        return carry

    lax.fori_loop(0, places, place, 0)

    def per_segment(seg, carry):
        count = count_ref[seg]

        def take(at, how_many):
            places_of = [list_ref[seg * places + at + i] for i in range(how_many)]
            found = [blocks_ref[p] for p in places_of]
            both = found[0] if how_many == 1 else jnp.concatenate(found, axis=0)
            absorb(seg, both[:, :head_dim], both[:, head_dim:], q_ref, m_ref, l_ref, acc_ref, scale)

        def quad(step, inner):
            take(4 * step, 4)
            return inner

        lax.fori_loop(0, count // 4, quad, 0)
        rest = count // 4 * 4

        @pl.when(count % 4 >= 2)
        def _():
            take(rest, 2)

        @pl.when(count % 2 == 1)
        def _():
            take(count - 1, 1)

        return carry

    lax.fori_loop(0, segs, per_segment, 0)


def own_kernel(scale, q_ref, own_ref, m_ref, l_ref, acc_ref):
    head_dim = q_ref.shape[1]
    seg_len = own_ref.shape[1]
    key_at = lax.broadcasted_iota(jnp.int32, (seg_len, TILE), 0)
    query_at = lax.broadcasted_iota(jnp.int32, (seg_len, TILE), 1) % seg_len
    causal = query_at >= key_at

    def own(seg, carry):
        keys, values = own_ref[seg, :, :head_dim], own_ref[seg, :, head_dim:]
        absorb(seg, keys, values, q_ref, m_ref, l_ref, acc_ref, scale, mask=causal, first=True)
        return carry

    lax.fori_loop(0, q_ref.shape[0], own, 0)


def carry_in(old, new):
    for source, target in zip(old, new):
        target[...] = source[...]


def chunk_kernel(scale, shared, seg_ref, q_ref, blocks_ref, m_in, l_in, acc_in, m_ref, l_ref, acc_ref, list_ref, count_ref):
    carry_in((m_in, l_in, acc_in), (m_ref, l_ref, acc_ref))
    absorb_blocks(seg_ref, blocks_ref, q_ref, m_ref, l_ref, acc_ref, list_ref, count_ref, scale)
    head_dim = q_ref.shape[1]

    def step(seg, carry):
        for at in range(0, len(shared), 4):
            found = jnp.concatenate([blocks_ref[p] for p in shared[at : at + 4]], axis=0)
            keys, values = found[:, :head_dim], found[:, head_dim:]
            absorb(seg, keys, values, q_ref, m_ref, l_ref, acc_ref, scale)
        return carry

    if shared:
        lax.fori_loop(0, q_ref.shape[0], step, 0)


def last_kernel(scale, seg_a_ref, seg_b_ref, x_ref, q_ref, blocks_a_ref, blocks_b_ref, m_in, l_in, acc_in, *refs):
    outs, (m_ref, l_ref, acc_ref, list_ref, count_ref) = refs[:-5], refs[-5:]
    carry_in((m_in, l_in, acc_in), (m_ref, l_ref, acc_ref))
    for seg_ref, blocks_ref in ((seg_a_ref, blocks_a_ref), (seg_b_ref, blocks_b_ref)):
        absorb_blocks(
            seg_ref, blocks_ref, q_ref, m_ref, l_ref, acc_ref, list_ref, count_ref, scale
        )
    seg_len = outs[0].shape[0]
    head_dim = q_ref.shape[1]
    group = q_ref.shape[2] // seg_len
    segs = q_ref.shape[0]

    for step, out_ref in enumerate(outs):
        seg = (x_ref[0] + step) % segs
        for g in range(group):
            cols = slice(g * seg_len, (g + 1) * seg_len)
            value = acc_ref[seg, :, cols] / l_ref[seg, :, cols]
            out_ref[:, g * head_dim : (g + 1) * head_dim] = value.T.astype(jnp.bfloat16)


def pick_kernel(sources, n_in, rows_ref, *refs):
    count = len(sources)
    inputs, outputs = refs[:n_in], refs[n_in : n_in + count]
    buffers, reads, write = refs[n_in + count : n_in + 2 * count], refs[-1 - count : -1], refs[-1]
    base = 0
    for names, buffer, read in zip(sources, buffers, reads):

        def start(at, carry, names=names, buffer=buffer, read=read, base=base):
            for inner, name in enumerate(names):
                place = at * len(names) + inner
                block = inputs[name].at[rows_ref[base + place]]
                pltpu.make_async_copy(block, buffer.at[place], read.at[at]).start()
            return carry

        lax.fori_loop(0, buffer.shape[0] // len(names), start, 0)
        base += buffer.shape[0]
    for number, (names, buffer, out_ref, read) in enumerate(zip(sources, buffers, outputs, reads)):

        def pass_on(at, carry, names=names, buffer=buffer, out_ref=out_ref, read=read, number=number):
            part = pl.ds(at * len(names), len(names))
            pltpu.make_async_copy(buffer.at[part], buffer.at[part], read.at[at]).wait()
            pltpu.make_async_copy(buffer.at[part], out_ref.at[part], write.at[number]).start()
            return carry

        lax.fori_loop(0, buffer.shape[0] // len(names), pass_on, 0)
    for number, (buffer, out_ref) in enumerate(zip(buffers, outputs)):
        pltpu.make_async_copy(buffer, out_ref, write.at[number]).wait()


def column_tiles(columns):
    return [slice(at, at + PROJECT_TILE) for at in range(0, columns, PROJECT_TILE)]


def times(rows, weight):
    return jnp.dot(rows, weight, preferred_element_type=jnp.float32)


def stage_kernel(rows_ref, weight_ref, *refs):
    fetched, (total_ref, *staged), (own_ref, sems) = refs[:3], refs[3:7], refs[7:]
    pairs = [(weight_ref, own_ref)] + list(zip(fetched, staged))
    copies = [pltpu.make_async_copy(a, b, sems.at[i]) for i, (a, b) in enumerate(pairs)]
    for copy in copies:
        copy.start()
    copies[0].wait()
    for tile in column_tiles(total_ref.shape[1]):
        total_ref[:, tile] = times(rows_ref[...], own_ref[:, tile])
    for copy in copies[1:]:
        copy.wait()


def sides_kernel(c_ref, total_ref, right_ref, left_ref, mine_ref, other_ref, out_ref):
    right, left = right_ref[...], left_ref[...]
    even = c_ref[0] == 0
    first, second = jnp.where(even, right, left), jnp.where(even, left, right)
    for tile in column_tiles(out_ref.shape[1]):
        out_ref[:, tile] = (
            total_ref[:, tile] + times(first, mine_ref[:, tile]) + times(second, other_ref[:, tile])
        )


def far_kernel(total_ref, rows_ref, weight_ref, out_ref, buffer_ref, sems):
    copies = []
    for i, tile in enumerate(column_tiles(out_ref.shape[1])):
        total = total_ref[:, tile] + times(rows_ref[...], weight_ref[:, tile])
        buffer_ref[:, tile] = total.astype(out_ref.dtype)
        copies.append(
            pltpu.make_async_copy(buffer_ref.at[:, tile], out_ref.at[:, tile], sems.at[i])
        )
        copies[-1].start()
    for copy in copies:
        copy.wait()


VMEM = pl.BlockSpec(memory_space=pltpu.VMEM)
SMEM = pl.BlockSpec(memory_space=pltpu.SMEM)
ANY = pl.BlockSpec(memory_space=pl.ANY)


def state_shapes(q):
    segs, head_dim, columns = q.shape
    return [
        jax.ShapeDtypeStruct((segs, 1, columns), jnp.float32),
        jax.ShapeDtypeStruct((segs, 1, columns), jnp.float32),
        jax.ShapeDtypeStruct((segs, head_dim, columns), jnp.float32),
    ]


def params():
    return pltpu.CompilerParams(vmem_limit_bytes=40 * 1024 * 1024)


def tables(places, segs):
    return [pltpu.SMEM((segs * places,), jnp.int32), pltpu.SMEM((segs,), jnp.int32)]


def attend_own(q, own, scale):
    return pl.pallas_call(
        functools.partial(own_kernel, scale),
        out_shape=state_shapes(q),
        in_specs=[VMEM, VMEM],
        out_specs=[VMEM] * 3,
        compiler_params=params(),
        cost_estimate=SMALL,
    )(q, own)


def attend_chunk(q, seg_of, blocks, state, scale, shared=()):
    return pl.pallas_call(
        functools.partial(chunk_kernel, scale, shared),
        out_shape=state_shapes(q),
        in_specs=[SMEM] + [VMEM] * 5,
        out_specs=[VMEM] * 3,
        scratch_shapes=tables(seg_of.shape[0], q.shape[0]),
        compiler_params=params(),
        cost_estimate=ATTEND,
    )(seg_of, q, blocks, *state)


def attend_last(q, fetched, state, x, scale):
    (seg_a, blocks_a), (seg_b, blocks_b) = fetched
    segs, head_dim, columns = q.shape
    seg_len = blocks_a.shape[1]
    group = columns // seg_len
    places = max(seg_a.shape[0], seg_b.shape[0])
    return pl.pallas_call(
        functools.partial(last_kernel, scale),
        out_shape=[jax.ShapeDtypeStruct((seg_len, group * head_dim), jnp.bfloat16)] * segs,
        in_specs=[SMEM] * 3 + [VMEM] * 6,
        out_specs=[VMEM] * segs,
        scratch_shapes=[pltpu.VMEM(s.shape, s.dtype) for s in state_shapes(q)]
        + tables(places, segs),
        compiler_params=params(),
        cost_estimate=ATTEND,
    )(seg_a, seg_b, x, q, blocks_a, blocks_b, *state)


def pick(plan, buffers, told=None):
    block, dtype = buffers[0].shape[1:], buffers[0].dtype
    names = tuple(n for n, _ in plan)
    sizes = [rows.size for _, rows in plan]
    out = pl.pallas_call(
        functools.partial(pick_kernel, names, len(buffers)),
        out_shape=[jax.ShapeDtypeStruct((size,) + block, dtype) for size in sizes],
        in_specs=[SMEM] + [ANY] * len(buffers),
        out_specs=[ANY] * len(plan),
        scratch_shapes=[pltpu.VMEM((size,) + block, dtype) for size in sizes]
        + [pltpu.SemaphoreType.DMA((size // len(n),)) for n, size in zip(names, sizes)]
        + [pltpu.SemaphoreType.DMA((len(plan),))],
        compiler_params=pltpu.CompilerParams(vmem_limit_bytes=56 * 1024 * 1024),
        cost_estimate=told or SMALL,
    )(jnp.concatenate([rows.reshape(-1) for _, rows in plan]), *buffers)
    return [x.reshape(rows.shape + block) for x, (_, rows) in zip(out, plan)]


def small_params(mebibytes):
    return pltpu.CompilerParams(vmem_limit_bytes=mebibytes * 1024 * 1024)


def stage(rows, own, fetched):
    total = jax.ShapeDtypeStruct((rows.shape[0], own.shape[1]), jnp.float32)
    return pl.pallas_call(
        stage_kernel,
        out_shape=[total] + [jax.ShapeDtypeStruct(w.shape, w.dtype) for w in fetched],
        in_specs=[VMEM] + [ANY] * 4,
        out_specs=[VMEM] * 4,
        scratch_shapes=[pltpu.VMEM(own.shape, own.dtype), pltpu.SemaphoreType.DMA((4,))],
        compiler_params=small_params(30),
        cost_estimate=SMALL,
    )(rows, own, *fetched)


def add_sides(c, total, right, left, mine, other):
    return pl.pallas_call(
        sides_kernel,
        out_shape=jax.ShapeDtypeStruct(total.shape, total.dtype),
        in_specs=[SMEM] + [VMEM] * 5,
        out_specs=VMEM,
        compiler_params=small_params(8),
        cost_estimate=SMALL,
    )(c, total, right, left, mine, other)


def add_far(total, rows, weight):
    return pl.pallas_call(
        far_kernel,
        out_shape=jax.ShapeDtypeStruct(total.shape, jnp.bfloat16),
        in_specs=[VMEM] * 3,
        out_specs=ANY,
        scratch_shapes=[
            pltpu.VMEM(total.shape, jnp.bfloat16),
            pltpu.SemaphoreType.DMA((total.shape[1] // PROJECT_TILE,)),
        ],
        compiler_params=small_params(8),
        cost_estimate=SMALL,
    )(total, rows, weight)


def together(*arrays):
    return lax.optimization_barrier(arrays)


def per_device(queries, new_kv, prompt_kv, pool, parents, lengths, location, out_weight):
    tok_rows = queries.shape[0]
    seg_dev, max_anc = parents.shape
    head_dim = prompt_kv.shape[1] // 2
    group = queries.shape[1] // head_dim
    seg_len = tok_rows // seg_dev
    blocks = pool.shape[0]
    scale = head_dim ** (-0.5)
    n_leaf = lax.axis_size("leaf")
    n_head = lax.axis_size("head")
    planes = n_leaf // LANES
    capacity = 2
    me = lax.axis_index("leaf")
    plane = me // LANES
    core = me % CORES

    def along_z(x, step):
        pairs = [(d, (d + step * LANES) % n_leaf) for d in range(n_leaf)]
        return lax.ppermute(x, "leaf", pairs)

    def along_x(x, step):
        return lax.ppermute(x, "head", [(d, (d + step) % n_head) for d in range(n_head)])

    def other_core(x):
        return lax.ppermute(x, "leaf", [(d, d ^ 1) for d in range(n_leaf)])

    in_plane = [[p * LANES + lane for lane in range(LANES)] for p in range(planes)]

    def spread(x):
        return lax.all_to_all(x, "leaf", 0, 0, tiled=True, axis_index_groups=in_plane)

    up1 = along_z(pool, 1)
    down1 = along_z(pool, -1)

    n_all = n_leaf * n_head

    def by_core(x):
        pairs = []
        for d in range(n_all):
            leaf, head = divmod(d, n_head)
            step = -1 if leaf % CORES == 0 else 1
            pairs.append((d, leaf * n_head + (head + step) % n_head))
        return lax.ppermute(x, ("leaf", "head"), pairs)

    weight1 = by_core(out_weight)

    slots = seg_dev * max_anc
    stored = location[parents].reshape(-1)
    live = (jnp.arange(max_anc)[None, :] < lengths[:, None]).reshape(-1)
    owner = jnp.where(live, stored // blocks, -1)
    row = stored % blocks
    order = jnp.arange(slots)
    rank = jnp.sum(
        (owner[:, None] == owner[None, :]) & (order[:, None] > order[None, :]), axis=1
    )
    dist = (plane - owner // LANES) % planes
    cell = jnp.where(live, (dist * LANES + owner % LANES) * capacity + rank, -1)
    hit = cell[None, :] == jnp.arange(n_leaf * capacity)[:, None]
    wanted = jnp.sum(jnp.where(hit, row[None, :], 0), axis=1).astype(jnp.int32)
    seg_of = jnp.sum(jnp.where(hit, (order // max_anc + 1)[None, :], 0), axis=1) - 1
    seg_of = seg_of.astype(jnp.int32).reshape(planes, LANES, capacity)
    per_lane = jnp.transpose(wanted.reshape(planes, LANES, capacity), (1, 0, 2))
    here = spread(per_lane.reshape(LANES, 1, planes * capacity))
    here = here.reshape(LANES, planes, capacity)

    q = jnp.transpose(
        queries.reshape(seg_dev, seg_len, group, head_dim), (0, 3, 2, 1)
    ).reshape(seg_dev, head_dim, group * seg_len)
    own = new_kv.reshape(seg_dev, seg_len, 2 * head_dim)
    state = attend_own(q, own, scale)
    here, *state = together(here, *state)

    def segs_at(dists, more=0):
        parts = [seg_of[d] for d in dists] + [jnp.full((LANES, more), -1, jnp.int32)] * bool(more)
        return jnp.concatenate(parts, axis=1).reshape(-1)

    def flat(x):
        return x.reshape((-1,) + x.shape[-2:])

    prompt_rows, width = prompt_kv.shape
    table = here.reshape(1, -1).astype(prompt_kv.dtype)
    table = jnp.pad(table, ((0, prompt_rows - 1), (0, width - table.shape[1])))
    notice = jnp.concatenate([prompt_kv, table], axis=0)
    same_lane = [[p * LANES + lane for p in range(planes)] for lane in range(LANES)]
    notices = lax.all_to_all(
        jnp.broadcast_to(notice[None], (planes,) + notice.shape),
        "leaf",
        0,
        0,
        tiled=True,
        axis_index_groups=same_lane,
    )
    notices, up1, down1 = together(notices, up1, down1)
    up2 = along_z(up1, 1)
    down2 = along_z(down1, -1)
    lane_prompt = notices[:, :prompt_rows].reshape(1, planes * prompt_rows, width)

    zero = jnp.zeros((LANES, 1), jnp.int32)
    rows01 = jnp.concatenate([here[:, 0], here[:, 1], here[:, planes - 1], zero], axis=1)
    plan01 = ((0, 0, 1, 1, 2, 2, 3), rows01)
    got01 = spread(pick([plan01], [pool, up1, down1, lane_prompt])[0])
    up2, down2, weight1, notices = together(up2, down2, weight1, notices)
    asked = notices[:, prompt_rows, : LANES * planes * capacity].astype(jnp.int32)
    asked = asked.reshape(planes, LANES, planes, capacity)
    asked = lax.dynamic_slice_in_dim(jnp.concatenate([asked, asked], axis=0), plane, planes, 0)
    weight2 = by_core(weight1)
    ask_up = asked[1, :, 3]
    ask_down = asked[planes - 1, :, planes - 3]
    on_core = (jnp.arange(LANES) % CORES)[:, None]
    ask_far = jnp.where(on_core == 0, asked[2, :, 4], asked[planes - 2, :, 4])
    rows2 = jnp.concatenate([here[:, 2], here[:, planes - 2], ask_far], axis=1)
    send_up, send_down, rest = pick(
        [
            ((0, 0), ask_up),
            ((1, 1), ask_down),
            ((0, 0, 1, 1, 0, 0, 0, 0, 1, 1, 1, 1), rows2),
        ],
        [up2, down2],
        LARGE,
    )
    up3 = along_z(send_up, 1)
    down3 = along_z(send_down, -1)
    rest, got01 = together(rest, got01)
    got2 = spread(rest)
    weight1_too = other_core(weight1)
    every = 3 * capacity + 1
    prompts = tuple(range(every - 1, LANES * every, every))
    state = attend_chunk(
        q, segs_at([0, 1, planes - 1], 1), flat(got01), state, scale, shared=prompts
    )

    up3, down3, *state = together(up3, down3, *state)
    reach = [(d, (d + (2 if d % CORES == 0 else -2) * LANES) % n_leaf) for d in range(n_leaf)]
    got4 = lax.ppermute(got2[:, 2 * capacity :], "leaf", reach)
    got3 = spread(jnp.concatenate([up3, down3], axis=1))
    state = attend_chunk(q, segs_at([2, planes - 2], capacity), flat(got2), state, scale)

    got3, got4, weight1_too, *state = together(got3, got4, weight1_too, *state)
    x = lax.axis_index("head").astype(jnp.int32).reshape(1)
    fetched = ((segs_at([3, planes - 3]), flat(got3)), (segs_at([4]), flat(got4)))
    keep, to_up, to_far, to_down = attend_last(q, fetched, state, x, scale)

    from_far = along_x(to_far, 2)
    from_down = along_x(to_up, 1)
    from_up = along_x(to_down, -1)
    c = core.astype(jnp.int32).reshape(1)
    total, mine, other, far = stage(keep, out_weight, (weight1, weight1_too, weight2))
    total = add_sides(c, total, from_up, from_down, mine, other)
    return add_far(total, from_far, far)


def solution(mesh):
    return jax.shard_map(
        per_device,
        mesh=mesh,
        in_specs=(
            P("leaf", "head"),
            P("leaf", "head"),
            P("leaf", "head"),
            P("leaf", None, "head"),
            P("leaf", None),
            P("leaf"),
            P(),
            P("head", None),
        ),
        out_specs=P(("leaf", "head"), None),
        check_vma=False,
    )
```
